32 devices in a mesh: horiz: 8 (over z, y), lev: 4 (over x, core).
Axes of the slice: x: 2, y: 2, z: 4, core: 2. Of those that a mesh axis runs over, the one named last changes fastest.
Arguments:
- control: float32 [64, 32, 4096], P('lev', None, 'horiz'), may hold values from -6 to 6
- members: bfloat16 [64, 4, 32, 4096], P('lev', None, None, 'horiz'), may hold values from -6 to 6
- extinction: float32 [4], replicated, may hold values from 0.5 to 2
- kernels: bfloat16 [4096, 64, 128], P('horiz', 'lev'), may hold values from 0 to 1
- innovation: bfloat16 [4096, 128], P('horiz'), may hold values from -16 to 16
- obs_weight: bfloat16 [4096, 128], P('horiz'), may hold values from 0.25 to 4
- owners: int32 [4096, 1], P('horiz'), may hold values from 0 to 7; in each aligned block of 512 rows (0 to 511, 512 to 1023, ...) at most 128 rows name the same one
- pixel_columns: int32 [4096, 128], P('horiz'), may hold values from 0 to 511
- pixel_counts: int32 [4096], P('horiz'), may hold values from 1 to 128
Outputs:
- gradient: float32 [64, 32, 4096], P('lev', None, 'horiz')
The draws below stay inside these ranges and needn't reach their ends.
Inputs may be any that keep to these rules, and one draw needn't show every extreme that they name: `owners`: among the 512 blocks of one index of horiz, no owner is named more than 128 times, and in some index's blocks one owner is named exactly 128 times.
All inputs are finite; a program needn't handle non-finite values.
Results may differ from the reference program's by a relative error of at most 0.0037.
Values may be sent and summed in bfloat16 or wider, within the bound.
A program may use at most 128 MiB of HBM per device.

```python
import math
import jax
import jax.numpy as jnp
import numpy as np
from jax import lax

LEV = 64
SPEC = 4
MEM = 32
BLK = 128
HALF = 4
COL_DEV = 512
OBS_DEV = 512
NCOL = 4096
NBLK = 4096
CAP = 128
N_HORIZ = 8


def set_ends(values, rng, smallest, top_value):
    index_at = [jax.random.randint(jax.random.fold_in(rng, axis), (), 0, length) for axis, length in enumerate(values.shape)]
    widest = values.shape.index(max(values.shape))
    neighbour = index_at[:widest] + [(index_at[widest] + 1) % values.shape[widest]] + index_at[widest + 1:]
    return values.at[tuple(index_at)].set(smallest).at[tuple(neighbour)].set(top_value)


def levels(key, shape, split, least, high):
    factor_of, own = 1.0, jax.random.fold_in(key, 6)
    for position, parts in split:
        steps = jnp.exp(jax.random.uniform(jax.random.fold_in(own, position), (parts,), jnp.float32, least / len(split), high / len(split)))
        factor_of = factor_of * jnp.repeat(steps, shape[position] // parts).reshape([-1 if axis == position else 1 for axis in range(len(shape))])
    return factor_of


def shared_out(own_key, own, number, rows, count, top, limit, skew):
    order = jax.random.permutation(own_key, count)
    crowded, common = portions_of(count, rows * top, limit, skew, True), portions_of(count, rows * top, limit, skew, False)
    places = jnp.arange(count)

    def named(lengths, rotation):
        used = int((lengths > 0).sum())
        fixed = max(1, used // 4)
        moved = fixed + (places - fixed + rotation * (used - fixed)) % max(1, count - fixed)
        return jnp.zeros((count,), jnp.int32).at[order[jnp.where(places < fixed, places, moved)]].set(jnp.asarray(lengths, jnp.int32))

    lengths = jnp.where(number % 4 == 0, named(crowded, number // 4), named(common, number - number // 4 - 1))
    mixed = jax.random.permutation(jax.random.fold_in(own, 3), count)
    donor, taker = mixed[0:count // 2 * 2:2], mixed[1:count // 2 * 2:2]
    slack = jnp.minimum(lengths[donor] - 1, limit - lengths[taker]) // 2
    slack = jnp.where((donor == order[0]) | (taker == order[0]) | (lengths[taker] == 0), 0, jnp.maximum(slack, 0))
    moved = jax.random.randint(jax.random.fold_in(own, 4), (count // 2,), 0, 1 << 20) % (slack + 1)
    lengths = lengths.at[donor].add(-moved).at[taker].add(moved)
    labels = jnp.searchsorted(jnp.cumsum(lengths), jnp.arange(rows * top), side="right").astype(jnp.int32)
    table = labels.reshape(top, rows).T
    table = table[jax.random.permutation(jax.random.fold_in(own, 1), rows)]
    rotation = jax.random.randint(jax.random.fold_in(own, 2), (rows, 1), 0, top)
    return jnp.take_along_axis(table, (jnp.arange(top)[None, :] + rotation) % top, axis=1)


def portions_of(count, total, reach, skew, full):
    loads = [(1 << 20) // math.isqrt(grade ** skew) + 1 for grade in range(1, count + 1)]
    largest = reach if full else min(reach, max(-(-total // count), total * loads[0] // sum(loads)))
    least = 1 if total - largest >= count - 1 else 0
    given, surplus = [largest] + [least] * (count - 1), total - largest - least * (count - 1)
    while surplus > 0:
        candidates = [i for i in range(1, count) if given[i] < largest] or [i for i in range(1, count) if given[i] < reach]
        pool, remaining = sum([loads[i] for i in candidates]), surplus
        for i in candidates:
            more = min(reach - given[i], max(1, remaining * loads[i] // pool), surplus)
            given[i] = given[i] + more
            surplus = surplus - more
    return np.array(given)


def centred(own_key, extent, scale, limit, pieces=(), held_as=jnp.bfloat16):
    values = scale * jax.random.normal(own_key, extent, jnp.float32)
    if pieces:
        values = values * levels(own_key, extent, pieces, -0.22, 0.18)
    return jnp.clip(values, -limit, limit).astype(held_as)


def setup_inputs(seed: int = 0) -> dict:
    streams_of = jax.random.split(jax.random.key(seed), 10)
    control = centred(streams_of[0], (LEV, MEM, NCOL), 1.0, 6.0, ((0, 4), (2, 8)), jnp.float32)
    members = centred(streams_of[1], (LEV, SPEC, MEM, NCOL), 1.0, 6.0, ((0, 4), (3, 8)))
    extinction = jnp.clip(jnp.exp(jax.random.uniform(streams_of[2], (SPEC,), jnp.float32, math.log(0.5), math.log(2.0))), 0.5, 2.0)
    kernels = jnp.clip(1.0 * jax.random.uniform(streams_of[3], (NBLK, LEV, BLK), jnp.float32) ** levels(streams_of[3], (NBLK, LEV, BLK), ((0, 8), (1, 4)), -0.2, 0.2), 0.0, 1.0).astype(jnp.bfloat16)
    innovation = centred(streams_of[4], (NBLK, BLK), 3.0, 16.0, ((0, 8),))
    obs_weight = jnp.clip(jnp.exp(math.log(4.0) - 2.7725887 * jax.random.uniform(streams_of[5], (NBLK, BLK), jnp.float32) ** levels(streams_of[5], (NBLK, BLK), ((0, 8),), -0.2, 0.2)), 0.25, 4.0).astype(jnp.bfloat16)
    owners_keys = jax.random.split(jax.random.fold_in(streams_of[6], 1), NBLK // OBS_DEV)
    owners_turns = jax.random.permutation(jax.random.fold_in(streams_of[6], 3), NBLK // OBS_DEV)
    owners = jax.vmap(lambda own, number: shared_out(jax.random.fold_in(streams_of[6], 2), own, number, OBS_DEV, N_HORIZ, 1, CAP, 2))(owners_keys, owners_turns).reshape((NBLK, 1))
    pixel_columns = set_ends(jax.random.randint(streams_of[7], (NBLK, BLK), 0, COL_DEV), jax.random.fold_in(streams_of[7], 1), 0, COL_DEV - 1).astype(jnp.int32)
    pixel_counts = set_ends(jax.random.randint(streams_of[8], (NBLK,), 1, BLK + 1), jax.random.fold_in(streams_of[8], 1), 1, BLK).astype(jnp.int32)
    return {"control": control, "members": members, "extinction": extinction, "kernels": kernels, "innovation": innovation, "obs_weight": obs_weight, "owners": owners, "pixel_columns": pixel_columns, "pixel_counts": pixel_counts}


def level_matrix():
    index_levels = jnp.arange(LEV, dtype=jnp.float32)
    spread = LEV / 8.0
    distance = index_levels[:, None] - index_levels[None, :]
    matrix = jnp.exp(-distance * distance / (2.0 * spread * spread)) / (2.5066283 * spread)
    return matrix.astype(jnp.bfloat16)

def column_taps():
    offsets = jnp.arange(2 * HALF + 1, dtype=jnp.float32) - HALF
    spread = HALF / 2.0
    weights = jnp.exp(-offsets * offsets / (2.0 * spread * spread))
    return weights / jnp.sum(weights)

def smooth_columns(values):
    tap_weights = column_taps()
    span = values.shape[2]
    padded = jnp.pad(values, ((0, 0), (0, 0), (HALF, HALF)))
    running = jnp.zeros(values.shape, jnp.float32)
    for offset in range(2 * HALF + 1):
        running = running + tap_weights[offset] * padded[:, :, offset:offset + span]
    return running

def reference(control, members, extinction, kernels, innovation, obs_weight, owners, pixel_columns, pixel_counts):
    level_loc = level_matrix().astype(jnp.float32)
    scale = 1.0 / math.sqrt(MEM)
    control_b = lax.optimization_barrier(control.astype(jnp.bfloat16)).astype(jnp.float32)
    vertical = jnp.einsum('ab,bmc->amc', level_loc, control_b, precision=lax.Precision.HIGHEST)
    increment = smooth_columns(vertical)
    mixed = jnp.einsum('s,asmc->amc', extinction.astype(jnp.float32), members.astype(jnp.float32), precision=lax.Precision.HIGHEST)
    column_field = lax.optimization_barrier(jnp.sum(mixed * increment, axis=1)) * scale
    target = (owners[:, 0][:, None] * COL_DEV + pixel_columns).astype(jnp.int32)
    picked = jnp.take(column_field, target, axis=1)
    kernel_values = kernels.astype(jnp.float32)
    evolved = lax.optimization_barrier(jnp.sum(kernel_values * jnp.transpose(picked, (1, 0, 2)), axis=1))
    live_pixels = jnp.arange(BLK, dtype=jnp.int32)[None, :] < pixel_counts[:, None]
    misfit = jnp.where(live_pixels, obs_weight.astype(jnp.float32) * (evolved - innovation.astype(jnp.float32)), 0.0)
    contrib = kernel_values * misfit[:, None, :]
    flat_terms = jnp.transpose(contrib, (0, 2, 1)).reshape(-1, LEV)
    field_grad = jax.ops.segment_sum(flat_terms, target.reshape(-1), num_segments=NCOL).T
    member_grad = mixed * field_grad[:, None, :] * scale
    smoothed = smooth_columns(member_grad)
    smoothed_b = lax.optimization_barrier(smoothed.astype(jnp.bfloat16)).astype(jnp.float32)
    return control + jnp.einsum('ba,bmc->amc', level_loc, smoothed_b, precision=lax.Precision.HIGHEST)
```

```python
import functools
import math

import jax
import jax.numpy as jnp
import numpy as np
from jax import lax
from jax.experimental import pallas as pl
from jax.experimental.pallas import tpu as pltpu
from jax.sharding import PartitionSpec as P

LEV = 64
HALF = 4
LANES = 128
PAIR = 16
GROUP = 64
BF = jnp.bfloat16
F32 = jnp.float32
MESH = pl.DeviceIdType.MESH
MIB = 1024 * 1024


def level_matrix():
    index_levels = np.arange(LEV, dtype=np.float32)
    spread = np.float32(LEV / 8.0)
    distance = index_levels[:, None] - index_levels[None, :]
    matrix = np.exp(-distance * distance / (2 * spread * spread)) / (np.float32(2.5066283) * spread)
    return matrix.astype(BF)


def column_taps():
    offsets = np.arange(2 * HALF + 1, dtype=np.float32) - HALF
    spread = np.float32(HALF / 2.0)
    weights = np.exp(-offsets * offsets / (2 * spread * spread))
    return weights / np.sum(weights)


def tap_matrix(width):
    rows = np.arange(width + LANES)
    place = np.where(rows < width + HALF, rows, rows - width - LANES)
    used = (rows < width + HALF) | (rows >= width + LANES - HALF)
    gap = place[:, None] - np.arange(width)[None, :]
    near = (np.abs(gap) <= HALF) & used[:, None]
    dense = np.where(near, column_taps()[np.clip(gap + HALF, 0, 2 * HALF)], 0.0).astype(np.float32)
    high = dense.astype(BF)
    low = (dense - high.astype(np.float32)).astype(BF)
    return high, low


def spread_levels(matrix):
    dense = np.kron(matrix.astype(np.float32), np.eye(PAIR, dtype=np.float32))
    return jnp.asarray(dense.astype(BF))


def dot(a, b):
    return jnp.dot(a, b, preferred_element_type=F32)


def greet(partners):
    barrier = pltpu.get_barrier_semaphore()
    for device in partners:
        pl.semaphore_signal(barrier, inc=1, device_id=device, device_id_type=MESH)
    pl.semaphore_wait(barrier, len(partners))


def remote(src, dst, send_sem, recv_sem, device):
    return pltpu.make_async_remote_copy(
        src_ref=src,
        dst_ref=dst,
        send_sem=send_sem,
        recv_sem=recv_sem,
        device_id=device,
        device_id_type=MESH,
    )


def send(*args):
    copy = remote(*args)
    copy.start()
    return copy


def fetch(src, dst, sem):
    copy = pltpu.make_async_copy(src, dst, sem)
    copy.start()
    return copy


def others(axis, count):
    me = lax.axis_index(axis)
    return [lax.rem(me + k, count) for k in range(1, count)]


def flip(index):
    return index + 1 - 2 * lax.rem(index, 2)


def front_kernel(
    levs,
    count,
    scale,
    ext_hbm,
    owner_hbm,
    control_hbm,
    members_hbm,
    kern_hbm,
    col_hbm,
    inn_hbm,
    w_hbm,
    cnt_hbm,
    kron_hbm,
    hi_hbm,
    lo_hbm,
    misfit_ref,
    mixed_all,
    ext_s,
    owner_s,
    control_v,
    members_v,
    kern_v,
    col_v,
    inn_v,
    w_v,
    cnt_v,
    kron_v,
    hi_v,
    lo_v,
    ctrl_all,
    mixed_v,
    halo_v,
    vert_v,
    field_all,
    field_v,
    part_v,
    slots,
    local_sem,
    ctl_sem,
    c_far,
    c_near,
    c_on,
    h_sem,
    z_sem,
    y_sem,
    t_sem,
    g_sem,
    m_far,
    m_near,
    m_on,
):
    levels, members, width = control_v.shape
    tiles = width // LANES
    halves = members // PAIR
    blocks = col_v.shape[0]
    rows = blocks // levs
    lev, me = lax.axis_index("lev"), lax.axis_index("horiz")
    near, far = flip(lev), lax.rem(lev + 2, levs)
    across = flip(far)
    right, left = lax.rem(me + 1, count), lax.rem(me + count - 1, count)
    own = pl.ds(pl.multiple_of(lev * levels, levels), levels)
    afar = pl.ds(pl.multiple_of(far * levels, levels), levels)
    mine = pl.ds(pl.multiple_of(lev * rows, rows), rows)

    tile_cols = [pl.ds(t * LANES, LANES) for t in range(tiles)]
    ctl = [
        fetch(control_hbm.at[:, :, c], control_v.at[:, :, c], ctl_sem.at[t])
        for t, c in enumerate(tile_cols)
    ]
    local = [
        fetch(src, dst, local_sem.at[k])
        for k, (src, dst) in enumerate(
            [
                (ext_hbm, ext_s),
                (members_hbm, members_v),
                (
                    kron_hbm.at[pl.ds(pl.multiple_of(lev * levels * PAIR, levels * PAIR), levels * PAIR)],
                    kron_v,
                ),
                (hi_hbm, hi_v),
                (lo_hbm, lo_v),
                (owner_hbm, owner_s),
                (kern_hbm, kern_v),
                (col_hbm, col_v),
                (inn_hbm.at[mine], inn_v),
                (w_hbm.at[mine], w_v),
                (cnt_hbm, cnt_v),
            ]
        )
    ]
    greet(
        [{"lev": side} for side in others("lev", levs)]
        + [{"horiz": peer} for peer in others("horiz", count)]
    )

    away, beside = [], []
    for t, c in enumerate(tile_cols):
        ctl[t].wait()
        for half in range(halves):
            ctrl_all[half, own, :, c] = control_v[:, pl.ds(half * PAIR, PAIR), c].astype(BF)
        block = ctrl_all.at[:, own, :, c]
        away.append(send(block, block, c_far.at[0, t], c_far.at[1, t], {"lev": far}))
        beside.append(send(block, block, c_near.at[0, t], c_near.at[1, t], {"lev": near}))

    local[0].wait()
    local[1].wait()

    def mix(t):
        total = ext_s[0] * members_v[:, 0, :, tile_cols[t]].astype(F32)
        for species in range(1, members_v.shape[1]):
            total = total + ext_s[species] * members_v[:, species, :, tile_cols[t]].astype(F32)
        mixed_v[:, :, tile_cols[t]] = total
        for half in range(halves):
            mixed_all[half, own, :, tile_cols[t]] = total[:, half * PAIR : (half + 1) * PAIR].astype(BF)

    mix(0)
    mix(tiles - 1)
    edges = [
        send(
            mixed_all.at[:, own, :, tile_cols[t]],
            halo_v.at[k],
            h_sem.at[0, k],
            h_sem.at[1, k],
            {"horiz": peer},
        )
        for k, (t, peer) in enumerate(((0, left), (tiles - 1, right)))
    ]
    for t in range(1, tiles - 1):
        mix(t)

    onward = []

    def pass_on(t):
        away[t].wait_recv()
        block = ctrl_all.at[:, afar, :, tile_cols[t]]
        onward.append(send(block, block, c_on.at[0, t], c_on.at[1, t], {"lev": near}))

    pass_on(0)
    for edge in edges:
        edge.wait()
    lane = lax.broadcasted_iota(jnp.int32, (1, 1, LANES), 2)
    after = HALF * jnp.where(me < count - 1, 1, 0)
    before = LANES - HALF * jnp.where(me > 0, 1, 0)
    for half in range(halves):
        halo = jnp.where(lane < after, halo_v[0, half].astype(F32), 0.0)
        halo = jnp.where(lane >= before, halo_v[1, half].astype(F32), halo)
        mixed_v[:, pl.ds(half * PAIR, PAIR), pl.ds(width, LANES)] = halo
        mixed_all[half, own, :, pl.ds(width, LANES)] = halo.astype(BF)

    local[2].wait()
    for t, c in enumerate(tile_cols):
        if t:
            pass_on(t)
        beside[t].wait_recv()
        onward[t].wait_recv()
        for half in range(halves):
            x = ctrl_all[half, :, :, c].reshape(LEV * PAIR, LANES)
            vert_v[half, :, c] = dot(kron_v[...], x).astype(BF)

    local[3].wait()
    local[4].wait()
    total = None
    for half in range(halves):
        v = vert_v[half]
        inc = dot(v, hi_v[...]) + dot(v, lo_v[...])
        inc = inc.reshape(levels, PAIR, width + LANES)
        term = jnp.sum(mixed_v[:, pl.ds(half * PAIR, PAIR), :] * inc, axis=1)
        total = term if total is None else total + term
    total = total * scale
    for t in range(tiles + 1):
        field_all[me, t] = total[:, t * LANES : (t + 1) * LANES].astype(BF)

    beyond = [lax.rem(me + 2 * k, count) for k in range(1, count // 2)]
    beyond_from = [lax.rem(me + count - 2 * k, count) for k in range(1, count // 2)]
    pair = flip(me)
    block = field_all.at[me]
    z_copies = [
        send(block, block, z_sem.at[0, k], z_sem.at[1, k], {"horiz": peer})
        for k, peer in enumerate(beyond)
    ]
    y_copies = [send(block, block, y_sem.at[0, 0], y_sem.at[1, 0], {"horiz": pair})]
    for k, peer in enumerate(beyond_from):
        z_copies[k].wait_recv()
        block = field_all.at[peer]
        y_copies.append(send(block, block, y_sem.at[0, k + 1], y_sem.at[1, k + 1], {"horiz": pair}))

    m_away, m_beside, m_onward = [], [], []
    for half in range(halves):
        block = mixed_all.at[half, own]
        m_away.append(send(block, block, m_far.at[0, half], m_far.at[1, half], {"lev": far}))
        m_beside.append(send(block, block, m_near.at[0, half], m_near.at[1, half], {"lev": near}))

    for copy in y_copies:
        copy.wait_recv()
    lane2 = lax.broadcasted_iota(jnp.int32, (levels, LANES), 1)
    for h in range(count):
        for t in range(tiles):
            value = field_all[h, t].astype(F32)
            if t == 0 and h > 0:
                value = value + jnp.where(lane2 < HALF, field_all[h - 1, tiles].astype(F32), 0.0)
            if t == tiles - 1 and h < count - 1:
                value = value + jnp.where(
                    lane2 >= LANES - HALF, field_all[h + 1, tiles].astype(F32), 0.0
                )
            field_v[h, t] = value

    for k in range(5, 8):
        local[k].wait()

    def one_peer(k, carry):
        peer = jnp.where(k == 0, far, jnp.where(k == 1, across, jnp.where(k == 2, near, lev)))
        start = pl.multiple_of(peer * rows, rows)

        def step(group, carry):
            base = pl.multiple_of(start + group * GROUP, GROUP)
            cols = col_v[pl.ds(base, GROUP), :]
            out = []
            for i in range(GROUP):
                owner = owner_s[base + i]
                col = jnp.broadcast_to(cols[i : i + 1, :], (levels, LANES))
                low = jnp.bitwise_and(col, LANES - 1)
                high = jnp.right_shift(col, 7)
                picked = jnp.take_along_axis(field_v[owner, 0], low, axis=1)
                for tile in range(1, tiles):
                    other = jnp.take_along_axis(field_v[owner, tile], low, axis=1)
                    picked = jnp.where(high == tile, other, picked)
                prod = picked * kern_v[base + i].astype(F32)
                out.append(jnp.sum(prod, axis=0, keepdims=True))
            part_v[pl.ds(base, GROUP), :] = jnp.concatenate(out, axis=0)
            return carry

        lax.fori_loop(0, rows // GROUP, step, 0)

        @pl.when(k < levs - 1)
        def _():
            remote(
                part_v.at[pl.ds(start, rows)], slots.at[k], t_sem.at[0, k], t_sem.at[1, k], {"lev": peer}
            ).start()

        return carry

    lax.fori_loop(0, levs, one_peer, 0)

    for half in range(halves):
        m_away[half].wait_recv()
        block = mixed_all.at[half, afar]
        m_onward.append(send(block, block, m_on.at[0, half], m_on.at[1, half], {"lev": near}))

    for k in range(8, 11):
        local[k].wait()
    counts = jnp.transpose(jnp.broadcast_to(cnt_v[pl.ds(lev, 1), :].astype(F32), (LANES, LANES)))
    live = lax.broadcasted_iota(jnp.int32, (rows, LANES), 1).astype(F32) < counts
    total = part_v[mine, :]
    sides = [far, across, near]
    for k, side in enumerate(sides):
        start = pl.multiple_of(side * rows, rows)
        copy = remote(
            part_v.at[pl.ds(start, rows)], slots.at[k], t_sem.at[0, k], t_sem.at[1, k], {"lev": side}
        )
        copy.wait()
        total = total + slots[k]
    misfit = w_v[...].astype(F32) * (total - inn_v[...].astype(F32)) * scale
    misfit_ref[mine, :] = jnp.where(live, misfit, 0.0).astype(BF)
    block = misfit_ref.at[mine]
    spread = [
        send(block, block, g_sem.at[0, k], g_sem.at[1, k], {"lev": side})
        for k, side in enumerate(sides)
    ]

    for copy in away + z_copies + y_copies + m_away:
        copy.wait_send()
    for copy in beside + onward:
        copy.wait_send()
    for copy in m_beside + m_onward + spread:
        copy.wait()


def adjoint_kernel(owner_ref, kern_ref, col_ref, mis_ref, out_ref, acc):
    blocks = col_ref.shape[0]
    levels = kern_ref.shape[1]
    count = acc.shape[0]
    tiles = acc.shape[2] // levels
    acc[...] = jnp.zeros_like(acc)
    lane_row = lax.broadcasted_iota(jnp.int32, (LANES, LANES), 0).astype(F32).astype(BF)
    one, zero = jnp.ones((), BF), jnp.zeros((), BF)

    def step(group, carry):
        base = pl.multiple_of(group * GROUP, GROUP)
        cols = col_ref[pl.ds(base, GROUP), :]
        low = jnp.bitwise_and(cols, LANES - 1).astype(F32)
        high = jnp.right_shift(cols, 7)
        misfit = mis_ref[pl.ds(base, GROUP), :].astype(F32)
        parts = [jnp.where(high == tile, misfit, 0.0) for tile in range(tiles)]
        for i in range(GROUP):
            owner = owner_ref[base + i]
            kern = kern_ref[base + i].astype(F32)
            rows = jnp.concatenate(
                [(kern * part[i : i + 1, :]).astype(BF) for part in parts], axis=0
            )
            row = jnp.broadcast_to(low[i : i + 1, :], (LANES, LANES)).astype(BF)
            hot = jnp.where(lane_row == row, one, zero)
            acc[owner] += lax.dot_general(
                hot, rows, (((1,), (1,)), ((), ())), preferred_element_type=F32
            )
        return carry

    lax.fori_loop(0, blocks // GROUP, step, 0)

    lane = lax.broadcasted_iota(jnp.int32, (levels, LANES), 1)
    sums = [jnp.transpose(acc[h]) for h in range(count)]
    for h in range(count):
        out_ref[h, pl.ds(0, tiles * levels)] = sums[h].astype(BF)
        edge = jnp.zeros((levels, LANES), F32)
        if h < count - 1:
            edge = jnp.where(lane < HALF, sums[h + 1][:levels], edge)
        if h > 0:
            edge = jnp.where(lane >= LANES - HALF, sums[h - 1][(tiles - 1) * levels :], edge)
        out_ref[h, pl.ds(tiles * levels, levels)] = edge.astype(BF)


def return_kernel(count, levs, x_ref, out_ref, slots, send_a, recv_a, send_b, recv_b):
    me, lev = lax.axis_index("horiz"), lax.axis_index("lev")
    peers = others("horiz", count)
    sides = others("lev", levs)
    greet([{"horiz": peer} for peer in peers] + [{"lev": side} for side in sides])
    copies = [
        send(x_ref.at[peer], slots.at[k], send_a.at[k], recv_a.at[k], {"horiz": peer})
        for k, peer in enumerate(peers)
    ]
    total = x_ref[me].astype(F32)
    for k, copy in enumerate(copies):
        copy.wait()
        total = total + slots[k].astype(F32)
    out_ref[lev] = total
    block = out_ref.at[lev]
    copies = [
        send(block, block, send_b.at[k], recv_b.at[k], {"lev": side})
        for k, side in enumerate(sides)
    ]
    for copy in copies:
        copy.wait()


def final_kernel(
    mixed_ref, fg_ref, kron_hbm, hi_ref, lo_ref, control_ref, out_ref, grad_v, kron_ref, sem
):
    levels, members, width = control_ref.shape
    size = levels * PAIR
    at = pl.multiple_of(lax.axis_index("lev") * size, size)
    kron_copy = fetch(kron_hbm.at[pl.ds(at, size)], kron_ref, sem)
    slabs = fg_ref.shape[0]
    tiles = width // LANES + 1
    for half in range(members // PAIR):
        for slab in range(slabs):
            for t in range(tiles):
                fg = fg_ref[slab, pl.ds(t * levels, levels), :]
                m = mixed_ref[half, pl.ds(slab * levels, levels), :, pl.ds(t * LANES, LANES)]
                grad = m.astype(F32) * fg[:, None, :]
                grad_v[pl.ds(slab * levels * PAIR, levels * PAIR), pl.ds(t * LANES, LANES)] = (
                    grad.astype(BF).reshape(levels * PAIR, LANES)
                )
        if half == 0:
            kron_copy.wait()
        mixed_levels = dot(kron_ref[...], grad_v[...])
        high = mixed_levels.astype(BF)
        low = (mixed_levels - high.astype(F32)).astype(BF)
        total = dot(high, hi_ref[...]) + dot(high, lo_ref[...]) + dot(low, hi_ref[...])
        part = pl.ds(half * PAIR, PAIR)
        out_ref[:, part, :] = control_ref[:, part, :] + total.reshape(levels, PAIR, width)


def vmem(count):
    return [pl.BlockSpec(memory_space=pltpu.VMEM)] * count


def smem(count):
    return [pl.BlockSpec(memory_space=pltpu.SMEM)] * count


def hbm(count):
    return [pl.BlockSpec(memory_space=pltpu.HBM)] * count


def pairs(*size):
    return pltpu.SemaphoreType.DMA((2,) + size)


def body(
    control,
    members,
    extinction,
    kernels,
    innovation,
    obs_weight,
    owners,
    pixel_columns,
    pixel_counts,
):
    levels, mem_count, width = control.shape
    blocks, _, pixels = kernels.shape
    count, levs = lax.axis_size("horiz"), lax.axis_size("lev")
    tiles = width // LANES
    halves = mem_count // PAIR
    rows = blocks // levs
    full = width + LANES
    kron_all = spread_levels(level_matrix())
    high, low = tap_matrix(width)
    hi, lo = jnp.asarray(high), jnp.asarray(low)
    hi_t, lo_t = jnp.asarray(high.T), jnp.asarray(low.T)
    scale = 1.0 / math.sqrt(mem_count)
    owner_ids = owners[:, 0]

    misfit, mixed_all = pl.pallas_call(
        functools.partial(front_kernel, levs, count, scale),
        out_shape=[
            jax.ShapeDtypeStruct((blocks, pixels), BF),
            jax.ShapeDtypeStruct((halves, levs * levels, PAIR, full), BF),
        ],
        in_specs=hbm(12),
        out_specs=vmem(2),
        scratch_shapes=[
            pltpu.SMEM(extinction.shape, F32),
            pltpu.SMEM(owner_ids.shape, jnp.int32),
            pltpu.VMEM(control.shape, F32),
            pltpu.VMEM(members.shape, BF),
            pltpu.VMEM(kernels.shape, BF),
            pltpu.VMEM(pixel_columns.shape, jnp.int32),
            pltpu.VMEM((rows, pixels), BF),
            pltpu.VMEM((rows, pixels), BF),
            pltpu.VMEM((levs, rows), jnp.int32),
            pltpu.VMEM((levels * PAIR, LEV * PAIR), BF),
            pltpu.VMEM((width, full), BF),
            pltpu.VMEM((width, full), BF),
            pltpu.VMEM((halves, levs * levels, PAIR, width), BF),
            pltpu.VMEM((levels, mem_count, full), F32),
            pltpu.VMEM((2, halves, levels, PAIR, LANES), BF),
            pltpu.VMEM((halves, levels * PAIR, width), BF),
            pltpu.VMEM((count, tiles + 1, levels, LANES), BF),
            pltpu.VMEM((count, tiles, levels, LANES), F32),
            pltpu.VMEM((blocks, pixels), F32),
            pltpu.VMEM((levs - 1, rows, pixels), F32),
            pltpu.SemaphoreType.DMA((11,)),
            pltpu.SemaphoreType.DMA((tiles,)),
            pairs(tiles),
            pairs(tiles),
            pairs(tiles),
            pairs(2),
            pairs(count // 2 - 1),
            pairs(count // 2),
            pairs(levs - 1),
            pairs(levs - 1),
            pairs(halves),
            pairs(halves),
            pairs(halves),
        ],
        compiler_params=pltpu.CompilerParams(
            vmem_limit_bytes=58 * MIB, collective_id=0, has_side_effects=True
        ),
    )(
        extinction,
        owner_ids,
        control,
        members,
        kernels,
        pixel_columns,
        innovation,
        obs_weight,
        pixel_counts.reshape(levs, rows),
        kron_all,
        hi_t,
        lo_t,
    )

    partial = pl.pallas_call(
        adjoint_kernel,
        out_shape=jax.ShapeDtypeStruct((count, (tiles + 1) * levels, LANES), BF),
        in_specs=smem(1) + vmem(3),
        out_specs=pl.BlockSpec(memory_space=pltpu.VMEM),
        scratch_shapes=[pltpu.VMEM((count, LANES, tiles * levels), F32)],
        compiler_params=pltpu.CompilerParams(vmem_limit_bytes=32 * MIB),
    )(owner_ids, kernels, pixel_columns, misfit)

    fg_all = pl.pallas_call(
        functools.partial(return_kernel, count, levs),
        out_shape=jax.ShapeDtypeStruct((levs, (tiles + 1) * levels, LANES), F32),
        in_specs=vmem(1),
        out_specs=pl.BlockSpec(memory_space=pltpu.VMEM),
        scratch_shapes=[pltpu.VMEM((count - 1, (tiles + 1) * levels, LANES), BF)]
        + [pltpu.SemaphoreType.DMA((count - 1,))] * 2
        + [pltpu.SemaphoreType.DMA((levs - 1,))] * 2,
        compiler_params=pltpu.CompilerParams(
            vmem_limit_bytes=32 * MIB, collective_id=1, has_side_effects=True
        ),
    )(partial)

    return pl.pallas_call(
        final_kernel,
        out_shape=jax.ShapeDtypeStruct(control.shape, F32),
        in_specs=vmem(2) + hbm(1) + vmem(3),
        out_specs=pl.BlockSpec(memory_space=pltpu.VMEM),
        scratch_shapes=[
            pltpu.VMEM((LEV * PAIR, full), BF),
            pltpu.VMEM((levels * PAIR, LEV * PAIR), BF),
            pltpu.SemaphoreType.DMA,
        ],
        compiler_params=pltpu.CompilerParams(vmem_limit_bytes=32 * MIB),
    )(mixed_all, fg_all, kron_all, hi, lo, control)


def solution(mesh):
    placed = (
        P("lev", None, "horiz"),
        P("lev", None, None, "horiz"),
        P(),
        P("horiz", "lev", None),
        P("horiz", None),
        P("horiz", None),
        P("horiz", None),
        P("horiz", None),
        P("horiz"),
    )
    return jax.shard_map(
        body, mesh=mesh, in_specs=placed, out_specs=P("lev", None, "horiz"), check_vma=False
    )
```

```python
import functools
import math

import jax
import jax.numpy as jnp
import numpy as np
from jax import lax
from jax.experimental import pallas as pl
from jax.experimental.pallas import tpu as pltpu
from jax.sharding import PartitionSpec as P

LEV = 64
HALF = 4
LANES = 128
PAIR = 16
GROUP = 64
BF = jnp.bfloat16
F32 = jnp.float32
MESH = pl.DeviceIdType.MESH
MIB = 1024 * 1024


def level_matrix():
    index_levels = np.arange(LEV, dtype=np.float32)
    spread = np.float32(LEV / 8.0)
    distance = index_levels[:, None] - index_levels[None, :]
    matrix = np.exp(-distance * distance / (2 * spread * spread)) / (np.float32(2.5066283) * spread)
    return matrix.astype(BF)


def column_taps():
    offsets = np.arange(2 * HALF + 1, dtype=np.float32) - HALF
    spread = np.float32(HALF / 2.0)
    weights = np.exp(-offsets * offsets / (2 * spread * spread))
    return weights / np.sum(weights)


def tap_matrix(width):
    rows = np.arange(width + LANES)
    place = np.where(rows < width + HALF, rows, rows - width - LANES)
    used = (rows < width + HALF) | (rows >= width + LANES - HALF)
    gap = place[:, None] - np.arange(width)[None, :]
    near = (np.abs(gap) <= HALF) & used[:, None]
    dense = np.where(near, column_taps()[np.clip(gap + HALF, 0, 2 * HALF)], 0.0).astype(np.float32)
    high = dense.astype(BF)
    low = (dense - high.astype(np.float32)).astype(BF)
    return high, low


def spread_levels(matrix):
    dense = np.kron(matrix.astype(np.float32), np.eye(PAIR, dtype=np.float32))
    return jnp.asarray(dense.astype(BF))


def dot(a, b):
    return jnp.dot(a, b, preferred_element_type=F32)


def greet(partners):
    barrier = pltpu.get_barrier_semaphore()
    for device in partners:
        pl.semaphore_signal(barrier, inc=1, device_id=device, device_id_type=MESH)
    pl.semaphore_wait(barrier, len(partners))


def remote(src, dst, send_sem, recv_sem, device):
    return pltpu.make_async_remote_copy(
        src_ref=src,
        dst_ref=dst,
        send_sem=send_sem,
        recv_sem=recv_sem,
        device_id=device,
        device_id_type=MESH,
    )


def send(*args):
    copy = remote(*args)
    copy.start()
    return copy


def fetch(src, dst, sem):
    copy = pltpu.make_async_copy(src, dst, sem)
    copy.start()
    return copy


def others(axis, count):
    me = lax.axis_index(axis)
    return [lax.rem(me + k, count) for k in range(1, count)]


def flip(index):
    return index + 1 - 2 * lax.rem(index, 2)


def front_kernel(
    levs,
    count,
    scale,
    ext_hbm,
    owner_hbm,
    control_hbm,
    members_hbm,
    kern_hbm,
    col_hbm,
    inn_hbm,
    w_hbm,
    cnt_hbm,
    kron_hbm,
    hi_hbm,
    lo_hbm,
    misfit_ref,
    mixed_all,
    ext_s,
    owner_s,
    control_v,
    members_v,
    kern_v,
    col_v,
    inn_v,
    w_v,
    cnt_v,
    kron_v,
    hi_v,
    lo_v,
    ctrl_all,
    mixed_v,
    mixed_own,
    halo_v,
    vert_v,
    field_all,
    field_v,
    part_v,
    part_b,
    slots,
    local_sem,
    ctl_sem,
    c_far,
    c_near,
    c_on,
    h_sem,
    f_sem,
    t_sem,
    g_sem,
    m_far,
    m_near,
    m_on,
    m_loc,
):
    levels, members, width = control_v.shape
    tiles = width // LANES
    halves = members // PAIR
    blocks = col_v.shape[0]
    rows = blocks // levs
    lev, me = lax.axis_index("lev"), lax.axis_index("horiz")
    near, far = flip(lev), lax.rem(lev + 2, levs)
    across = flip(far)
    right, left = lax.rem(me + 1, count), lax.rem(me + count - 1, count)
    own = pl.ds(pl.multiple_of(lev * levels, levels), levels)
    afar = pl.ds(pl.multiple_of(far * levels, levels), levels)
    mine = pl.ds(pl.multiple_of(lev * rows, rows), rows)

    tile_cols = [pl.ds(t * LANES, LANES) for t in range(tiles)]
    ctl = [
        fetch(control_hbm.at[:, :, c], control_v.at[:, :, c], ctl_sem.at[t])
        for t, c in enumerate(tile_cols)
    ]
    local = [
        fetch(src, dst, local_sem.at[k])
        for k, (src, dst) in enumerate(
            [
                (ext_hbm, ext_s),
                (members_hbm, members_v),
                (
                    kron_hbm.at[pl.ds(pl.multiple_of(lev * levels * PAIR, levels * PAIR), levels * PAIR)],
                    kron_v,
                ),
                (hi_hbm, hi_v),
                (lo_hbm, lo_v),
                (owner_hbm, owner_s),
                (kern_hbm, kern_v),
                (col_hbm, col_v),
                (inn_hbm.at[mine], inn_v),
                (w_hbm.at[mine], w_v),
                (cnt_hbm, cnt_v),
            ]
        )
    ]
    greet(
        [{"lev": side} for side in others("lev", levs)]
        + [{"horiz": peer} for peer in others("horiz", count)]
    )

    away, beside = [], []
    for t, c in enumerate(tile_cols):
        ctl[t].wait()
        for half in range(halves):
            ctrl_all[half, own, :, c] = control_v[:, pl.ds(half * PAIR, PAIR), c].astype(BF)
        block = ctrl_all.at[:, own, :, c]
        away.append(send(block, block, c_far.at[0, t], c_far.at[1, t], {"lev": far}))
        beside.append(send(block, block, c_near.at[0, t], c_near.at[1, t], {"lev": near}))

    local[0].wait()
    local[1].wait()

    def mix(t):
        total = ext_s[0] * members_v[:, 0, :, tile_cols[t]].astype(F32)
        for species in range(1, members_v.shape[1]):
            total = total + ext_s[species] * members_v[:, species, :, tile_cols[t]].astype(F32)
        mixed_v[:, :, tile_cols[t]] = total
        for half in range(halves):
            mixed_own[half, :, :, tile_cols[t]] = total[:, half * PAIR : (half + 1) * PAIR].astype(BF)

    mix(0)
    mix(tiles - 1)
    edges = [
        send(
            mixed_own.at[:, :, :, tile_cols[t]],
            halo_v.at[k],
            h_sem.at[0, k],
            h_sem.at[1, k],
            {"horiz": peer},
        )
        for k, (t, peer) in enumerate(((0, left), (tiles - 1, right)))
    ]
    for t in range(1, tiles - 1):
        mix(t)

    onward = []

    def pass_on(t):
        away[t].wait_recv()
        block = ctrl_all.at[:, afar, :, tile_cols[t]]
        onward.append(send(block, block, c_on.at[0, t], c_on.at[1, t], {"lev": near}))

    pass_on(0)
    for edge in edges:
        edge.wait()
    lane = lax.broadcasted_iota(jnp.int32, (1, 1, LANES), 2)
    after = HALF * jnp.where(me < count - 1, 1, 0)
    before = LANES - HALF * jnp.where(me > 0, 1, 0)
    for half in range(halves):
        halo = jnp.where(lane < after, halo_v[0, half].astype(F32), 0.0)
        halo = jnp.where(lane >= before, halo_v[1, half].astype(F32), halo)
        mixed_v[:, pl.ds(half * PAIR, PAIR), pl.ds(width, LANES)] = halo
        mixed_own[half, :, :, pl.ds(width, LANES)] = halo.astype(BF)

    m_away, m_beside, m_onward, m_kept = [], [], [], []
    local[2].wait()
    for t, c in enumerate(tile_cols):
        if t:
            pass_on(t)
        if t == tiles - 1:
            for half in range(halves):
                block, place = mixed_own.at[half], mixed_all.at[half, own]
                m_away.append(send(block, place, m_far.at[0, half], m_far.at[1, half], {"lev": far}))
                m_beside.append(
                    send(block, place, m_near.at[0, half], m_near.at[1, half], {"lev": near})
                )
                m_kept.append(fetch(block, place, m_loc.at[half]))
        beside[t].wait_recv()
        onward[t].wait_recv()
        for half in range(halves):
            x = ctrl_all[half, :, :, c].reshape(LEV * PAIR, LANES)
            vert_v[half, :, c] = dot(kron_v[...], x).astype(BF)

    local[3].wait()
    local[4].wait()
    total = None
    for half in range(halves):
        v = vert_v[half]
        inc = dot(v, hi_v[...]) + dot(v, lo_v[...])
        inc = inc.reshape(levels, PAIR, width + LANES)
        term = jnp.sum(mixed_v[:, pl.ds(half * PAIR, PAIR), :] * inc, axis=1)
        total = term if total is None else total + term
    total = total * scale
    for t in range(tiles + 1):
        field_all[me, t] = total[:, t * LANES : (t + 1) * LANES].astype(BF)

    block = field_all.at[me]
    f_copies = [
        send(block, block, f_sem.at[0, k], f_sem.at[1, k], {"horiz": peer})
        for k, peer in enumerate(others("horiz", count))
    ]
    for copy in f_copies:
        copy.wait_recv()
    lane2 = lax.broadcasted_iota(jnp.int32, (levels, LANES), 1)
    for h in range(count):
        for t in range(tiles):
            value = field_all[h, t].astype(F32)
            if t == 0 and h > 0:
                value = value + jnp.where(lane2 < HALF, field_all[h - 1, tiles].astype(F32), 0.0)
            if t == tiles - 1 and h < count - 1:
                value = value + jnp.where(
                    lane2 >= LANES - HALF, field_all[h + 1, tiles].astype(F32), 0.0
                )
            field_v[h, t] = value

    for k in range(5, 8):
        local[k].wait()

    def one_peer(k, carry):
        peer = jnp.where(k == 0, far, jnp.where(k == 1, across, jnp.where(k == 2, near, lev)))
        start = pl.multiple_of(peer * rows, rows)

        def step(group, carry):
            base = pl.multiple_of(start + group * GROUP, GROUP)
            cols = col_v[pl.ds(base, GROUP), :]
            out = []
            for i in range(GROUP):
                owner = owner_s[base + i]
                col = jnp.broadcast_to(cols[i : i + 1, :], (levels, LANES))
                low = jnp.bitwise_and(col, LANES - 1)
                high = jnp.right_shift(col, 7)
                picked = jnp.take_along_axis(field_v[owner, 0], low, axis=1)
                for tile in range(1, tiles):
                    other = jnp.take_along_axis(field_v[owner, tile], low, axis=1)
                    picked = jnp.where(high == tile, other, picked)
                prod = picked * kern_v[base + i].astype(F32)
                out.append(jnp.sum(prod, axis=0, keepdims=True))
            rows_sum = jnp.concatenate(out, axis=0)
            part_v[pl.ds(base, GROUP), :] = rows_sum
            part_b[pl.ds(base, GROUP), :] = rows_sum.astype(BF)
            return carry

        lax.fori_loop(0, rows // GROUP, step, 0)

        @pl.when(k < levs - 1)
        def _():
            remote(
                part_b.at[pl.ds(start, rows)], slots.at[k], t_sem.at[0, k], t_sem.at[1, k], {"lev": peer}
            ).start()

        return carry

    lax.fori_loop(0, levs, one_peer, 0)

    for half in range(halves):
        m_away[half].wait_recv()
        block = mixed_all.at[half, afar]
        m_onward.append(send(block, block, m_on.at[0, half], m_on.at[1, half], {"lev": near}))

    for k in range(8, 11):
        local[k].wait()
    counts = jnp.transpose(jnp.broadcast_to(cnt_v[pl.ds(lev, 1), :].astype(F32), (LANES, LANES)))
    live = lax.broadcasted_iota(jnp.int32, (rows, LANES), 1).astype(F32) < counts
    total = part_v[mine, :]
    sides = [far, across, near]
    for k, side in enumerate(sides):
        start = pl.multiple_of(side * rows, rows)
        copy = remote(
            part_b.at[pl.ds(start, rows)], slots.at[k], t_sem.at[0, k], t_sem.at[1, k], {"lev": side}
        )
        copy.wait()
        total = total + slots[k].astype(F32)
    misfit = w_v[...].astype(F32) * (total - inn_v[...].astype(F32)) * scale
    misfit_ref[mine, :] = jnp.where(live, misfit, 0.0).astype(BF)
    block = misfit_ref.at[mine]
    spread = [
        send(block, block, g_sem.at[0, k], g_sem.at[1, k], {"lev": side})
        for k, side in enumerate(sides)
    ]

    for copy in away + f_copies + m_away:
        copy.wait_send()
    for copy in beside + onward:
        copy.wait_send()
    for copy in m_beside + m_onward + m_kept + spread:
        copy.wait()


def adjoint_kernel(owner_ref, kern_ref, col_ref, mis_ref, out_ref, acc):
    blocks = col_ref.shape[0]
    levels = kern_ref.shape[1]
    count = acc.shape[0]
    tiles = acc.shape[2] // levels
    acc[...] = jnp.zeros_like(acc)
    lane_row = lax.broadcasted_iota(jnp.int32, (LANES, LANES), 0).astype(F32).astype(BF)
    one, zero = jnp.ones((), BF), jnp.zeros((), BF)

    def step(group, carry):
        base = pl.multiple_of(group * GROUP, GROUP)
        cols = col_ref[pl.ds(base, GROUP), :]
        low = jnp.bitwise_and(cols, LANES - 1).astype(F32)
        high = jnp.right_shift(cols, 7)
        misfit = mis_ref[pl.ds(base, GROUP), :].astype(F32)
        parts = [jnp.where(high == tile, misfit, 0.0) for tile in range(tiles)]
        for i in range(GROUP):
            owner = owner_ref[base + i]
            kern = kern_ref[base + i].astype(F32)
            rows = jnp.concatenate(
                [(kern * part[i : i + 1, :]).astype(BF) for part in parts], axis=0
            )
            row = jnp.broadcast_to(low[i : i + 1, :], (LANES, LANES)).astype(BF)
            hot = jnp.where(lane_row == row, one, zero)
            acc[owner] += lax.dot_general(
                hot, rows, (((1,), (1,)), ((), ())), preferred_element_type=F32
            )
        return carry

    lax.fori_loop(0, blocks // GROUP, step, 0)

    lane = lax.broadcasted_iota(jnp.int32, (levels, LANES), 1)
    sums = [jnp.transpose(acc[h]) for h in range(count)]
    for h in range(count):
        out_ref[h, pl.ds(0, tiles * levels)] = sums[h].astype(BF)
        edge = jnp.zeros((levels, LANES), F32)
        if h < count - 1:
            edge = jnp.where(lane < HALF, sums[h + 1][:levels], edge)
        if h > 0:
            edge = jnp.where(lane >= LANES - HALF, sums[h - 1][(tiles - 1) * levels :], edge)
        out_ref[h, pl.ds(tiles * levels, levels)] = edge.astype(BF)


def back_kernel(
    count,
    levs,
    x_ref,
    mixed_hbm,
    kron_hbm,
    hi_hbm,
    lo_hbm,
    out_ref,
    mixed_v,
    kron_v,
    hi_v,
    lo_v,
    fg_v,
    levels_v,
    slots,
    r_sem,
    a_sem,
    local_sem,
):
    levels, members, width = out_ref.shape
    halves = members // PAIR
    size = levels * PAIR
    tiles = width // LANES + 1
    me, lev = lax.axis_index("horiz"), lax.axis_index("lev")
    near, far = flip(lev), lax.rem(lev + 2, levs)
    across = flip(far)
    at = pl.multiple_of(lev * size, size)
    local = [
        fetch(src, dst, local_sem.at[k])
        for k, (src, dst) in enumerate(
            [
                (mixed_hbm, mixed_v),
                (kron_hbm.at[pl.ds(at, size)], kron_v),
                (hi_hbm, hi_v),
                (lo_hbm, lo_v),
            ]
        )
    ]
    peers = others("horiz", count)
    sides = [near, far, across]
    greet([{"horiz": peer} for peer in peers] + [{"lev": side} for side in sides])
    reduce = [
        send(x_ref.at[peer], slots.at[k], r_sem.at[0, k], r_sem.at[1, k], {"horiz": peer})
        for k, peer in enumerate(peers)
    ]
    total = x_ref[me].astype(F32)
    for k, copy in enumerate(reduce):
        copy.wait_recv()
        total = total + slots[k].astype(F32)
    fg_v[lev] = total
    block = fg_v.at[lev]
    spread = [
        send(block, block, a_sem.at[0, k], a_sem.at[1, k], {"lev": side})
        for k, side in enumerate(sides)
    ]
    for copy in local:
        copy.wait()

    def slab(index, first):
        start = pl.multiple_of(index * levels, levels)
        begin = pl.multiple_of(index * size, size)
        for half in range(halves):
            columns = []
            for t in range(tiles):
                fg = fg_v[index, pl.ds(t * levels, levels), :]
                m = mixed_v[half, pl.ds(start, levels), :, pl.ds(t * LANES, LANES)]
                grad = m.astype(F32) * fg[:, None, :]
                columns.append(grad.astype(BF).reshape(size, LANES))
            term = dot(kron_v[:, pl.ds(begin, size)], jnp.concatenate(columns, axis=1))
            levels_v[half] = term if first else levels_v[half] + term

    slab(lev, True)
    for k, side in enumerate(sides):
        spread[k].wait_recv()
        slab(side, False)
    for half in range(halves):
        mixed_levels = levels_v[half]
        high = mixed_levels.astype(BF)
        low = (mixed_levels - high.astype(F32)).astype(BF)
        total = dot(high, hi_v[...]) + dot(high, lo_v[...]) + dot(low, hi_v[...])
        out_ref[:, pl.ds(half * PAIR, PAIR), :] = total.reshape(levels, PAIR, width)
    for copy in reduce + spread:
        copy.wait_send()


def vmem(count):
    return [pl.BlockSpec(memory_space=pltpu.VMEM)] * count


def smem(count):
    return [pl.BlockSpec(memory_space=pltpu.SMEM)] * count


def hbm(count):
    return [pl.BlockSpec(memory_space=pltpu.HBM)] * count


def pairs(*size):
    return pltpu.SemaphoreType.DMA((2,) + size)


def body(
    control,
    members,
    extinction,
    kernels,
    innovation,
    obs_weight,
    owners,
    pixel_columns,
    pixel_counts,
):
    levels, mem_count, width = control.shape
    blocks, _, pixels = kernels.shape
    count, levs = lax.axis_size("horiz"), lax.axis_size("lev")
    tiles = width // LANES
    halves = mem_count // PAIR
    rows = blocks // levs
    full = width + LANES
    kron_all = spread_levels(level_matrix())
    high, low = tap_matrix(width)
    hi, lo = jnp.asarray(high), jnp.asarray(low)
    hi_t, lo_t = jnp.asarray(high.T), jnp.asarray(low.T)
    scale = 1.0 / math.sqrt(mem_count)
    owner_ids = owners[:, 0]

    misfit, mixed_all = pl.pallas_call(
        functools.partial(front_kernel, levs, count, scale),
        out_shape=[
            jax.ShapeDtypeStruct((blocks, pixels), BF),
            jax.ShapeDtypeStruct((halves, levs * levels, PAIR, full), BF),
        ],
        in_specs=hbm(12),
        out_specs=vmem(1) + hbm(1),
        scratch_shapes=[
            pltpu.SMEM(extinction.shape, F32),
            pltpu.SMEM(owner_ids.shape, jnp.int32),
            pltpu.VMEM(control.shape, F32),
            pltpu.VMEM(members.shape, BF),
            pltpu.VMEM(kernels.shape, BF),
            pltpu.VMEM(pixel_columns.shape, jnp.int32),
            pltpu.VMEM((rows, pixels), BF),
            pltpu.VMEM((rows, pixels), BF),
            pltpu.VMEM((levs, rows), jnp.int32),
            pltpu.VMEM((levels * PAIR, LEV * PAIR), BF),
            pltpu.VMEM((width, full), BF),
            pltpu.VMEM((width, full), BF),
            pltpu.VMEM((halves, levs * levels, PAIR, width), BF),
            pltpu.VMEM((levels, mem_count, full), F32),
            pltpu.VMEM((halves, levels, PAIR, full), BF),
            pltpu.VMEM((2, halves, levels, PAIR, LANES), BF),
            pltpu.VMEM((halves, levels * PAIR, width), BF),
            pltpu.VMEM((count, tiles + 1, levels, LANES), BF),
            pltpu.VMEM((count, tiles, levels, LANES), F32),
            pltpu.VMEM((blocks, pixels), F32),
            pltpu.VMEM((blocks, pixels), BF),
            pltpu.VMEM((levs - 1, rows, pixels), BF),
            pltpu.SemaphoreType.DMA((11,)),
            pltpu.SemaphoreType.DMA((tiles,)),
            pairs(tiles),
            pairs(tiles),
            pairs(tiles),
            pairs(2),
            pairs(count - 1),
            pairs(levs - 1),
            pairs(levs - 1),
            pairs(halves),
            pairs(halves),
            pairs(halves),
            pltpu.SemaphoreType.DMA((halves,)),
        ],
        compiler_params=pltpu.CompilerParams(
            vmem_limit_bytes=58 * MIB, collective_id=0, has_side_effects=True
        ),
    )(
        extinction,
        owner_ids,
        control,
        members,
        kernels,
        pixel_columns,
        innovation,
        obs_weight,
        pixel_counts.reshape(levs, rows),
        kron_all,
        hi_t,
        lo_t,
    )

    partial = pl.pallas_call(
        adjoint_kernel,
        out_shape=jax.ShapeDtypeStruct((count, (tiles + 1) * levels, LANES), BF),
        in_specs=smem(1) + vmem(3),
        out_specs=pl.BlockSpec(memory_space=pltpu.VMEM),
        scratch_shapes=[pltpu.VMEM((count, LANES, tiles * levels), F32)],
        compiler_params=pltpu.CompilerParams(vmem_limit_bytes=32 * MIB),
    )(owner_ids, kernels, pixel_columns, misfit)

    delta = pl.pallas_call(
        functools.partial(back_kernel, count, levs),
        out_shape=jax.ShapeDtypeStruct(control.shape, F32),
        in_specs=vmem(1) + hbm(4),
        out_specs=pl.BlockSpec(memory_space=pltpu.VMEM),
        scratch_shapes=[
            pltpu.VMEM(mixed_all.shape, BF),
            pltpu.VMEM((levels * PAIR, LEV * PAIR), BF),
            pltpu.VMEM((full, width), BF),
            pltpu.VMEM((full, width), BF),
            pltpu.VMEM((levs, (tiles + 1) * levels, LANES), F32),
            pltpu.VMEM((halves, levels * PAIR, full), F32),
            pltpu.VMEM((count - 1, (tiles + 1) * levels, LANES), BF),
            pairs(count - 1),
            pairs(levs - 1),
            pltpu.SemaphoreType.DMA((4,)),
        ],
        compiler_params=pltpu.CompilerParams(
            vmem_limit_bytes=48 * MIB, collective_id=1, has_side_effects=True
        ),
    )(partial, mixed_all, kron_all, hi, lo)
    return control + delta


def solution(mesh):
    placed = (
        P("lev", None, "horiz"),
        P("lev", None, None, "horiz"),
        P(),
        P("horiz", "lev", None),
        P("horiz", None),
        P("horiz", None),
        P("horiz", None),
        P("horiz", None),
        P("horiz"),
    )
    return jax.shard_map(
        body, mesh=mesh, in_specs=placed, out_specs=P("lev", None, "horiz"), check_vma=False
    )
```

```python
import functools
import math

import jax
import jax.numpy as jnp
import numpy as np
from jax import lax
from jax.experimental import pallas as pl
from jax.experimental.pallas import tpu as pltpu
from jax.sharding import PartitionSpec as P

LEV = 64
HALF = 4
LANES = 128
PAIR = 16
GROUP = 128
MANY = 128
BF = jnp.bfloat16
F32 = jnp.float32
MESH = pl.DeviceIdType.MESH
MIB = 1024 * 1024


def level_matrix():
    index_levels = np.arange(LEV, dtype=np.float32)
    spread = np.float32(LEV / 8.0)
    distance = index_levels[:, None] - index_levels[None, :]
    matrix = np.exp(-distance * distance / (2 * spread * spread)) / (np.float32(2.5066283) * spread)
    return matrix.astype(BF)


def column_taps():
    offsets = np.arange(2 * HALF + 1, dtype=np.float32) - HALF
    spread = np.float32(HALF / 2.0)
    weights = np.exp(-offsets * offsets / (2 * spread * spread))
    return weights / np.sum(weights)


def tap_matrix(width):
    rows = np.arange(width + LANES)
    place = np.where(rows < width + HALF, rows, rows - width - 2 * HALF)
    used = rows < width + 2 * HALF
    gap = place[:, None] - np.arange(width)[None, :]
    near = (np.abs(gap) <= HALF) & used[:, None]
    dense = np.where(near, column_taps()[np.clip(gap + HALF, 0, 2 * HALF)], 0.0).astype(np.float32)
    high = dense.astype(BF)
    low = (dense - high.astype(np.float32)).astype(BF)
    return high, low


def spread_levels(matrix):
    dense = np.kron(matrix.astype(np.float32), np.eye(PAIR, dtype=np.float32))
    return jnp.asarray(dense.astype(BF))


def dot(a, b):
    return jnp.dot(a, b, preferred_element_type=F32)


def greet(partners):
    barrier = pltpu.get_barrier_semaphore()
    for device in partners:
        pl.semaphore_signal(barrier, inc=1, device_id=device, device_id_type=MESH)
    return lambda: pl.semaphore_wait(barrier, len(partners))


def remote(src, dst, send_sem, recv_sem, device):
    return pltpu.make_async_remote_copy(
        src_ref=src,
        dst_ref=dst,
        send_sem=send_sem,
        recv_sem=recv_sem,
        device_id=device,
        device_id_type=MESH,
    )


def send(*args):
    copy = remote(*args)
    copy.start()
    return copy


def fetch(src, dst, sem):
    copy = pltpu.make_async_copy(src, dst, sem)
    copy.start()
    return copy


def others(axis, count):
    me = lax.axis_index(axis)
    return [lax.rem(me + k, count) for k in range(1, count)]


def flip(index):
    return index + 1 - 2 * lax.rem(index, 2)


def pack_edge(lane, part, shift):
    total = None
    for level in range(PAIR):
        moved = pltpu.roll(part(level), (2 * HALF * level + shift) % LANES, 1)
        total = moved if total is None else jnp.where(jnp.right_shift(lane, 3) == level, moved, total)
    return total


def unpack_edge(lane, packed, level):
    moved = pltpu.roll(packed, (LANES - 2 * HALF * level) % LANES, 1)
    return jnp.where(lane < 2 * HALF, moved, 0.0)


def front_kernel(
    levs,
    count,
    scale,
    ext_hbm,
    owner_hbm,
    control_hbm,
    members_hbm,
    kern_hbm,
    col_hbm,
    inn_hbm,
    w_hbm,
    cnt_hbm,
    kron_hbm,
    hi_hbm,
    lo_hbm,
    misfit_ref,
    mixed_all,
    edge_all,
    ext_s,
    owner_s,
    control_v,
    members_v,
    kern_v,
    col_v,
    inn_v,
    w_v,
    cnt_v,
    kron_v,
    hi_v,
    lo_v,
    ctrl_all,
    ctrl_edge,
    mixed_v,
    mixed_own,
    edge_own,
    edge_out,
    edge_in,
    vert_v,
    field_all,
    field_v,
    part_v,
    chip_v,
    near_in,
    cross_out,
    cross_in,
    local_sem,
    ctl_sem,
    c_far,
    c_near,
    c_on,
    h_sem,
    f_sem,
    n_sem,
    x_sem,
    y_sem,
    m_far,
    m_near,
    m_on,
    m_loc,
):
    levels, members, width = control_v.shape
    tiles = width // LANES
    halves = members // PAIR
    blocks = col_v.shape[0]
    rows = blocks // levs
    lev, me = lax.axis_index("lev"), lax.axis_index("horiz")
    near, far = flip(lev), lax.rem(lev + 2, levs)
    across = flip(far)
    right, left = lax.rem(me + 1, count), lax.rem(me + count - 1, count)
    own = pl.ds(pl.multiple_of(lev * levels, levels), levels)
    afar = pl.ds(pl.multiple_of(far * levels, levels), levels)
    side, part = lax.rem(lev, 2), rows // 2

    tile_cols = [pl.ds(t * LANES, LANES) for t in range(tiles)]
    half_rows = [pl.ds(half * PAIR, PAIR) for half in range(halves)]
    all_here = greet(
        [{"lev": side} for side in others("lev", levs)]
        + [{"horiz": peer} for peer in others("horiz", count)]
    )
    ctl = [
        fetch(control_hbm.at[:, :, c], control_v.at[:, :, c], ctl_sem.at[t])
        for t, c in enumerate(tile_cols)
    ]
    away, beside, onward = {}, {}, {}

    def share(t, block):
        away[t] = send(block, block, c_far.at[0, t], c_far.at[1, t], {"lev": far})
        beside[t] = send(block, block, c_near.at[0, t], c_near.at[1, t], {"lev": near})

    def pass_on(t, block):
        away[t].wait_recv()
        onward[t] = send(block, block, c_on.at[0, t], c_on.at[1, t], {"lev": near})

    def share_tile(t):
        for half in range(halves):
            ctrl_all[half, own, :, tile_cols[t]] = control_v[:, half_rows[half], tile_cols[t]].astype(BF)
        share(t, ctrl_all.at[:, own, :, tile_cols[t]])

    lane = lax.broadcasted_iota(jnp.int32, (PAIR, LANES), 1)
    low_lane = jnp.bitwise_and(lane, 2 * HALF - 1)
    after = HALF * jnp.where(me < count - 1, 1, 0)
    before = HALF * jnp.where(me > 0, 1, 0)

    def send_edges(which, source):
        first, last = source.at[:, :, tile_cols[0]], source.at[:, :, tile_cols[tiles - 1]]
        copies = []
        for side, (view, shift, peer) in enumerate(((first, 0, left), (last, 2 * HALF, right))):
            for half in range(halves):
                packed = pack_edge(lane, lambda level: view[level, half_rows[half], :], shift)
                edge_out[which, side, half] = packed.astype(BF)
            copies.append(
                send(
                    edge_out.at[which, side],
                    edge_in.at[which, side],
                    h_sem.at[0, which, side],
                    h_sem.at[1, which, side],
                    {"horiz": peer},
                )
            )
        return copies

    def merged_edge(which, half):
        edge = jnp.where(low_lane < after, edge_in[which, 0, half].astype(F32), 0.0)
        return jnp.where(
            (low_lane >= HALF) & (low_lane < HALF + before),
            edge_in[which, 1, half].astype(F32),
            edge,
        ).astype(BF)

    early = tiles // 2
    all_here()
    ctl[0].wait()
    share_tile(0)
    local = [
        fetch(src, dst, local_sem.at[k])
        for k, (src, dst) in enumerate(
            [
                (ext_hbm, ext_s),
                (members_hbm, members_v),
                (
                    kron_hbm.at[pl.ds(pl.multiple_of(lev * levels * PAIR, levels * PAIR), levels * PAIR)],
                    kron_v,
                ),
                (hi_hbm, hi_v),
                (lo_hbm, lo_v),
                (owner_hbm, owner_s),
                (kern_hbm, kern_v),
                (col_hbm, col_v),
                (inn_hbm, inn_v),
                (w_hbm, w_v),
                (cnt_hbm, cnt_v),
            ]
        )
    ]
    for t in range(1, tiles):
        ctl[t].wait()
        if t < early:
            share_tile(t)
    control_edges = send_edges(0, control_v)

    local[0].wait()
    local[1].wait()
    for t in range(tiles):
        total = ext_s[0] * members_v[:, 0, :, tile_cols[t]].astype(F32)
        for species in range(1, members_v.shape[1]):
            total = total + ext_s[species] * members_v[:, species, :, tile_cols[t]].astype(F32)
        mixed_v[:, :, tile_cols[t]] = total
        for half in range(halves):
            mixed_own[half, :, :, tile_cols[t]] = total[:, half * PAIR : (half + 1) * PAIR].astype(BF)
    mixed_edges = send_edges(1, mixed_v)

    for copy in control_edges:
        copy.wait_recv()
    for half in range(halves):
        ctrl_edge[lev, half] = merged_edge(0, half)
    share(tiles, ctrl_edge.at[lev])
    for t in range(early, tiles):
        share_tile(t)
    for copy in mixed_edges:
        copy.wait_recv()
    for half in range(halves):
        edge_own[half] = merged_edge(1, half)

    for k in range(2, 5):
        local[k].wait()

    def raise_tile(t):
        pass_on(t, ctrl_all.at[:, afar, :, tile_cols[t]])
        if t == tiles - 1:
            start_mixed()
        beside[t].wait_recv()
        onward[t].wait_recv()
        for half in range(halves):
            x = ctrl_all[half, :, :, tile_cols[t]].reshape(LEV * PAIR, LANES)
            vert_v[half, :, tile_cols[t]] = dot(kron_v[...], x).astype(BF)

    def raise_edge():
        pass_on(tiles, ctrl_edge.at[far])
        beside[tiles].wait_recv()
        onward[tiles].wait_recv()
        for half in range(halves):
            x = []
            for slab in range(levs):
                packed = ctrl_edge[slab, half].astype(F32)
                x += [unpack_edge(lane, packed, level).astype(BF) for level in range(levels)]
            x = jnp.concatenate(x, axis=0)
            vert_v[half, :, pl.ds(width, LANES)] = dot(kron_v[...], x).astype(BF)

    m_away, m_beside, m_onward, m_kept = [], [], [], []

    def start_mixed():
        parts = [(mixed_own.at[half], mixed_all.at[half, own]) for half in range(halves)]
        parts.append((edge_own, edge_all.at[lev]))
        for k, (block, place) in enumerate(parts):
            m_away.append(send(block, place, m_far.at[0, k], m_far.at[1, k], {"lev": far}))
            m_beside.append(send(block, place, m_near.at[0, k], m_near.at[1, k], {"lev": near}))
            m_kept.append(fetch(block, place, m_loc.at[k]))

    f_copies = {}

    def make_field(t):
        spans = [pl.ds(max(t - 1, 0) * LANES, (min(t + 2, tiles) - max(t - 1, 0)) * LANES)]
        if t in (0, tiles - 1):
            spans.append(pl.ds(width, LANES))
        total = None
        for half in range(halves):
            inc = None
            for cols in spans:
                v = vert_v[half, :, cols]
                term = dot(v, hi_v[cols, tile_cols[t]]) + dot(v, lo_v[cols, tile_cols[t]])
                inc = term if inc is None else inc + term
            inc = inc.reshape(levels, PAIR, LANES)
            term = jnp.sum(mixed_v[:, half_rows[half], tile_cols[t]] * inc, axis=1)
            total = term if total is None else total + term
        field_all[me, t] = (total * scale).astype(BF)

    def send_field(group):
        block = field_all.at[me, pl.ds(group[0], len(group))]
        f_copies[group] = [
            send(
                block, block, f_sem.at[0, group[0], k], f_sem.at[1, group[0], k], {"horiz": peer}
            )
            for k, peer in enumerate(others("horiz", count))
        ]

    def take_field(group):
        for copy in f_copies[group]:
            copy.wait_recv()
        for t in group:
            for h in range(count):
                field_v[h, t] = field_all[h, t].astype(F32)

    def forward(peer, chosen, first):
        start = pl.multiple_of(peer * rows, rows)

        def step(group, carry):
            base = pl.multiple_of(start + group * GROUP, GROUP)
            cols = col_v[pl.ds(base, GROUP), :]
            out = []
            for i in range(GROUP):
                owner = owner_s[base + i]
                col = jnp.broadcast_to(cols[i : i + 1, :], (levels, LANES))
                low = jnp.bitwise_and(col, LANES - 1)
                high = jnp.right_shift(col, 7)
                picked = 0.0
                for tile in chosen:
                    value = jnp.take_along_axis(field_v[owner, tile], low, axis=1)
                    picked = jnp.where(high == tile, value, picked)
                prod = picked * kern_v[base + i].astype(F32)
                out.append(jnp.sum(prod, axis=0, keepdims=True))
            value = jnp.concatenate(out, axis=0)
            if not first:
                value = value + part_v[pl.ds(base, GROUP), :]
            part_v[pl.ds(base, GROUP), :] = value
            return carry

        lax.fori_loop(0, rows // GROUP, step, 0)

    def forward_all(chosen, first):
        lax.fori_loop(0, levs, lambda k, carry: (forward(k, chosen, first), carry)[1], 0)

    one, two = tuple(range(early)), tuple(range(early, tiles))
    raise_tile(0)
    raise_edge()
    raise_tile(1)
    make_field(0)
    for k in range(5, 8):
        local[k].wait()
    for t in range(2, tiles):
        raise_tile(t)
        make_field(t - 1)
        if t == early:
            send_field(one)
    make_field(tiles - 1)
    send_field(two)
    take_field(one)
    forward_all(one, True)
    take_field(two)

    def span(k):
        return pl.ds(pl.multiple_of(k * rows, rows), rows)

    def near_copy(k):
        return remote(
            part_v.at[span(k)], near_in.at[k], n_sem.at[0, k], n_sem.at[1, k], {"lev": near}
        )

    def cross_copy(k):
        return remote(
            cross_out.at[k], cross_in.at[k, side], x_sem.at[0, k], x_sem.at[1, k], {"lev": far}
        )

    def hand_copy(k):
        block = cross_in.at[k, side]
        return remote(block, block, y_sem.at[0, k], y_sem.at[1, k], {"lev": near})

    def sum_chip(k):
        near_copy(k).wait_recv()
        chip_v[span(k), :] = part_v[span(k), :] + near_in[k]
        own_part = pl.ds(pl.multiple_of(k * rows + side * part, part), part)
        cross_out[k] = chip_v[own_part, :].astype(BF)
        cross_copy(k).start()

    def hand_on(k):
        cross_copy(k).wait_recv()
        hand_copy(k).start()

    def one_part(k, carry):
        forward(k, two, False)
        near_copy(k).start()

        @pl.when(k >= 1)
        def _():
            sum_chip(k - 1)

        @pl.when(k >= 3)
        def _():
            hand_on(k - 3)

        return carry

    lax.fori_loop(0, levs, one_part, 0)
    sum_chip(levs - 1)

    for k in range(8, 11):
        local[k].wait()

    lane_row = lax.broadcasted_iota(jnp.int32, (rows, LANES), 1).astype(F32)
    for k in range(levs):
        if k >= levs - 3:
            hand_on(k)
    places = [mixed_all.at[half, afar] for half in range(halves)] + [edge_all.at[far]]
    for k, place in enumerate(places):
        m_away[k].wait_recv()
        m_onward.append(send(place, place, m_on.at[0, k], m_on.at[1, k], {"lev": near}))
    for k in range(levs):
        hand_copy(k).wait_recv()
        other = jnp.concatenate([cross_in[k, 0], cross_in[k, 1]], axis=0).astype(F32)
        evolved = chip_v[pl.ds(k * rows, rows), :] + other
        block = pl.ds(k * rows, rows)
        misfit = w_v[block, :].astype(F32) * (evolved - inn_v[block, :].astype(F32)) * scale
        counts = jnp.broadcast_to(cnt_v[pl.ds(k, 1), :].astype(F32), (LANES, LANES))
        live = lane_row < jnp.transpose(counts)
        misfit_ref[block, :] = jnp.where(live, misfit, 0.0).astype(BF)

    for k in range(levs):
        near_copy(k).wait_send()
        cross_copy(k).wait_send()
        hand_copy(k).wait_send()
    for copies in f_copies.values():
        for copy in copies:
            copy.wait_send()
    for group in (away, beside, onward):
        for copy in group.values():
            copy.wait_send()
    for copy in control_edges + mixed_edges + m_away:
        copy.wait_send()
    for copy in m_beside + m_onward + m_kept:
        copy.wait()


def adjoint_kernel(owner_ref, kern_ref, col_ref, mis_ref, out_ref, acc):
    blocks = col_ref.shape[0]
    levels = kern_ref.shape[1]
    count = acc.shape[0]
    tiles = acc.shape[2] // levels
    acc[...] = jnp.zeros_like(acc)
    lane_row = lax.broadcasted_iota(jnp.int32, (LANES, LANES), 0).astype(F32).astype(BF)
    one, zero = jnp.ones((), BF), jnp.zeros((), BF)

    def step(group, carry):
        base = pl.multiple_of(group * MANY, MANY)
        cols = col_ref[pl.ds(base, MANY), :]
        low = jnp.bitwise_and(cols, LANES - 1).astype(F32)
        high = jnp.right_shift(cols, 7)
        misfit = mis_ref[pl.ds(base, MANY), :].astype(F32)
        parts = [jnp.where(high == tile, misfit, 0.0) for tile in range(tiles)]
        for i in range(MANY):
            owner = owner_ref[base + i]
            kern = kern_ref[base + i]
            rows = jnp.concatenate(
                [
                    kern * jnp.broadcast_to(part[i : i + 1, :], (levels, LANES)).astype(BF)
                    for part in parts
                ],
                axis=0,
            )
            row = jnp.broadcast_to(low[i : i + 1, :], (LANES, LANES)).astype(BF)
            hot = jnp.where(lane_row == row, one, zero)
            acc[owner] += lax.dot_general(
                hot, rows, (((1,), (1,)), ((), ())), preferred_element_type=F32
            )
        return carry

    lax.fori_loop(0, blocks // MANY, step, 0)

    lane = lax.broadcasted_iota(jnp.int32, (levels, LANES), 1)
    sums = [jnp.transpose(acc[h]) for h in range(count)]
    for h in range(count):
        out_ref[h, pl.ds(0, tiles * levels)] = sums[h].astype(BF)
        edge = jnp.zeros((levels, LANES), F32)
        if h < count - 1:
            edge = jnp.where(lane < HALF, sums[h + 1][:levels], edge)
        if h > 0:
            moved = pltpu.roll(sums[h - 1][(tiles - 1) * levels :], 2 * HALF, 1)
            edge = jnp.where((lane >= HALF) & (lane < 2 * HALF), moved, edge)
        out_ref[h, pl.ds(tiles * levels, levels)] = edge.astype(BF)


def back_kernel(
    count,
    levs,
    x_ref,
    mixed_hbm,
    edge_hbm,
    kron_hbm,
    out_ref,
    mixed_v,
    edge_v,
    kron_v,
    fg_v,
    slots,
    r_sem,
    a_sem,
    local_sem,
):
    halves, size, full = out_ref.shape
    levels = size // PAIR
    tiles = full // LANES
    early = (tiles - 1) // 2
    groups = [range(early), range(early, tiles)]
    rows = [pl.ds(group[0] * levels, len(group) * levels) for group in groups]
    me, lev = lax.axis_index("horiz"), lax.axis_index("lev")
    near, far = flip(lev), lax.rem(lev + 2, levs)
    sides = [near, far, flip(far)]
    peers = others("horiz", count)
    greet([{"horiz": peer} for peer in peers] + [{"lev": side} for side in sides])()
    reduce = [
        [
            send(
                x_ref.at[peer, part],
                slots.at[k, part],
                r_sem.at[0, g, k],
                r_sem.at[1, g, k],
                {"horiz": peer},
            )
            for k, peer in enumerate(peers)
        ]
        for g, part in enumerate(rows)
    ]
    at = pl.multiple_of(lev * size, size)
    local = [
        fetch(mixed_hbm, mixed_v, local_sem.at[0]),
        fetch(edge_hbm, edge_v, local_sem.at[1]),
        fetch(kron_hbm.at[pl.ds(at, size)], kron_v, local_sem.at[2]),
    ]
    lane = lax.broadcasted_iota(jnp.int32, (PAIR, LANES), 1)

    def total_up(g):
        part = rows[g]
        total = x_ref[me, part].astype(F32)
        for k, copy in enumerate(reduce[g]):
            copy.wait_recv()
            total = total + slots[k, part].astype(F32)
        fg_v[lev, part] = total
        block = fg_v.at[lev, part]
        return [
            send(block, block, a_sem.at[0, g, k], a_sem.at[1, g, k], {"lev": side})
            for k, side in enumerate(sides)
        ]

    def slab(index, g, first):
        start = pl.multiple_of(index * levels, levels)
        begin = pl.multiple_of(index * size, size)
        group = groups[g]
        span = pl.ds(group[0] * LANES, len(group) * LANES)
        for half in range(halves):
            columns = []
            for t in group:
                fg = fg_v[index, pl.ds(t * levels, levels), :]
                if t < tiles - 1:
                    m = mixed_v[half, pl.ds(start, levels), :, pl.ds(t * LANES, LANES)]
                    grad = (m.astype(F32) * fg[:, None, :]).astype(BF).reshape(size, LANES)
                else:
                    packed = edge_v[index, half].astype(F32)
                    grad = jnp.concatenate(
                        [
                            (unpack_edge(lane, packed, level) * fg[level : level + 1, :]).astype(BF)
                            for level in range(levels)
                        ],
                        axis=0,
                    )
                columns.append(grad)
            term = dot(kron_v[:, pl.ds(begin, size)], jnp.concatenate(columns, axis=1))
            out_ref[half, :, span] = term if first else out_ref[half, :, span] + term

    spread = [total_up(0)]
    for copy in local:
        copy.wait()
    slab(lev, 0, True)
    spread.append(total_up(1))
    slab(lev, 1, True)
    for g in range(2):
        for k, side in enumerate(sides):
            spread[g][k].wait_recv()
            slab(side, g, False)
    for copies in reduce + spread:
        for copy in copies:
            copy.wait_send()


def final_kernel(levels_ref, hi_ref, lo_ref, control_ref, out_hbm, out_v, sem):
    levels, members, width = control_ref.shape
    copies = []
    for half in range(members // PAIR):
        part = pl.ds(half * PAIR, PAIR)
        mixed_levels = levels_ref[half]
        high = mixed_levels.astype(BF)
        low = (mixed_levels - high.astype(F32)).astype(BF)
        total = dot(high, hi_ref[...]) + dot(high, lo_ref[...]) + dot(low, hi_ref[...])
        out_v[half] = control_ref[:, part, :] + total.reshape(levels, PAIR, width)
        copies.append(fetch(out_v.at[half], out_hbm.at[:, part, :], sem.at[half]))
    for copy in copies:
        copy.wait()


def vmem(count):
    return [pl.BlockSpec(memory_space=pltpu.VMEM)] * count


def smem(count):
    return [pl.BlockSpec(memory_space=pltpu.SMEM)] * count


def hbm(count):
    return [pl.BlockSpec(memory_space=pltpu.HBM)] * count


def pairs(*size):
    return pltpu.SemaphoreType.DMA((2,) + size)


def body(
    control,
    members,
    extinction,
    kernels,
    innovation,
    obs_weight,
    owners,
    pixel_columns,
    pixel_counts,
):
    levels, mem_count, width = control.shape
    blocks, _, pixels = kernels.shape
    count, levs = lax.axis_size("horiz"), lax.axis_size("lev")
    tiles = width // LANES
    halves = mem_count // PAIR
    rows = blocks // levs
    full = width + LANES
    kron_all = spread_levels(level_matrix())
    high, low = tap_matrix(width)
    hi, lo = jnp.asarray(high), jnp.asarray(low)
    scale = 1.0 / math.sqrt(mem_count)
    owner_ids = owners[:, 0]

    misfit, mixed_all, edge_all = pl.pallas_call(
        functools.partial(front_kernel, levs, count, scale),
        out_shape=[
            jax.ShapeDtypeStruct((blocks, pixels), BF),
            jax.ShapeDtypeStruct((halves, levs * levels, PAIR, width), BF),
            jax.ShapeDtypeStruct((levs, halves, PAIR, LANES), BF),
        ],
        in_specs=hbm(12),
        out_specs=vmem(1) + hbm(2),
        scratch_shapes=[
            pltpu.SMEM(extinction.shape, F32),
            pltpu.SMEM(owner_ids.shape, jnp.int32),
            pltpu.VMEM(control.shape, F32),
            pltpu.VMEM(members.shape, BF),
            pltpu.VMEM(kernels.shape, BF),
            pltpu.VMEM(pixel_columns.shape, jnp.int32),
            pltpu.VMEM((blocks, pixels), BF),
            pltpu.VMEM((blocks, pixels), BF),
            pltpu.VMEM((levs, rows), jnp.int32),
            pltpu.VMEM((levels * PAIR, LEV * PAIR), BF),
            pltpu.VMEM((full, width), BF),
            pltpu.VMEM((full, width), BF),
            pltpu.VMEM((halves, levs * levels, PAIR, width), BF),
            pltpu.VMEM((levs, halves, PAIR, LANES), BF),
            pltpu.VMEM((levels, mem_count, width), F32),
            pltpu.VMEM((halves, levels, PAIR, width), BF),
            pltpu.VMEM((halves, PAIR, LANES), BF),
            pltpu.VMEM((2, 2, halves, PAIR, LANES), BF),
            pltpu.VMEM((2, 2, halves, PAIR, LANES), BF),
            pltpu.VMEM((halves, levels * PAIR, full), BF),
            pltpu.VMEM((count, tiles, levels, LANES), BF),
            pltpu.VMEM((count, tiles, levels, LANES), F32),
            pltpu.VMEM((blocks, pixels), F32),
            pltpu.VMEM((blocks, pixels), F32),
            pltpu.VMEM((levs, rows, pixels), F32),
            pltpu.VMEM((levs, rows // 2, pixels), BF),
            pltpu.VMEM((levs, 2, rows // 2, pixels), BF),
            pltpu.SemaphoreType.DMA((11,)),
            pltpu.SemaphoreType.DMA((tiles,)),
            pairs(tiles + 1),
            pairs(tiles + 1),
            pairs(tiles + 1),
            pairs(2, 2),
            pairs(tiles, count - 1),
            pairs(levs),
            pairs(levs),
            pairs(levs),
            pairs(halves + 1),
            pairs(halves + 1),
            pairs(halves + 1),
            pltpu.SemaphoreType.DMA((halves + 1,)),
        ],
        compiler_params=pltpu.CompilerParams(
            vmem_limit_bytes=58 * MIB, collective_id=0, has_side_effects=True
        ),
    )(
        extinction,
        owner_ids,
        control,
        members,
        kernels,
        pixel_columns,
        innovation,
        obs_weight,
        pixel_counts.reshape(levs, rows),
        kron_all,
        hi,
        lo,
    )

    partial = pl.pallas_call(
        adjoint_kernel,
        out_shape=jax.ShapeDtypeStruct((count, (tiles + 1) * levels, LANES), BF),
        in_specs=smem(1) + vmem(3),
        out_specs=pl.BlockSpec(memory_space=pltpu.VMEM),
        scratch_shapes=[pltpu.VMEM((count, LANES, tiles * levels), F32)],
        compiler_params=pltpu.CompilerParams(vmem_limit_bytes=32 * MIB),
    )(owner_ids, kernels, pixel_columns, misfit)

    levels_mixed = pl.pallas_call(
        functools.partial(back_kernel, count, levs),
        out_shape=jax.ShapeDtypeStruct((halves, levels * PAIR, full), F32),
        in_specs=vmem(1) + hbm(3),
        out_specs=pl.BlockSpec(memory_space=pltpu.VMEM),
        scratch_shapes=[
            pltpu.VMEM(mixed_all.shape, BF),
            pltpu.VMEM(edge_all.shape, BF),
            pltpu.VMEM((levels * PAIR, LEV * PAIR), BF),
            pltpu.VMEM((levs, (tiles + 1) * levels, LANES), F32),
            pltpu.VMEM((count - 1, (tiles + 1) * levels, LANES), BF),
            pairs(2, count - 1),
            pairs(2, levs - 1),
            pltpu.SemaphoreType.DMA((3,)),
        ],
        compiler_params=pltpu.CompilerParams(
            vmem_limit_bytes=50 * MIB, collective_id=1, has_side_effects=True
        ),
    )(partial, mixed_all, edge_all, kron_all)

    return pl.pallas_call(
        final_kernel,
        out_shape=jax.ShapeDtypeStruct(control.shape, F32),
        in_specs=vmem(4),
        out_specs=pl.BlockSpec(memory_space=pltpu.HBM),
        scratch_shapes=[
            pltpu.VMEM((halves, levels, PAIR, width), F32),
            pltpu.SemaphoreType.DMA((halves,)),
        ],
        compiler_params=pltpu.CompilerParams(vmem_limit_bytes=32 * MIB),
    )(levels_mixed, hi, lo, control)


def solution(mesh):
    placed = (
        P("lev", None, "horiz"),
        P("lev", None, None, "horiz"),
        P(),
        P("horiz", "lev", None),
        P("horiz", None),
        P("horiz", None),
        P("horiz", None),
        P("horiz", None),
        P("horiz"),
    )
    return jax.shard_map(
        body, mesh=mesh, in_specs=placed, out_specs=P("lev", None, "horiz"), check_vma=False
    )
```

```python
import functools
import math

import jax
import jax.numpy as jnp
import numpy as np
from jax import lax
from jax.experimental import pallas as pl
from jax.experimental.pallas import tpu as pltpu
from jax.sharding import PartitionSpec as P

LEV = 64
HALF = 4
LANES = 128
PAIR = 16
GROUP = 128
MANY = 128
BF = jnp.bfloat16
F32 = jnp.float32
MESH = pl.DeviceIdType.MESH
MIB = 1024 * 1024


def level_matrix():
    index_levels = np.arange(LEV, dtype=np.float32)
    spread = np.float32(LEV / 8.0)
    distance = index_levels[:, None] - index_levels[None, :]
    matrix = np.exp(-distance * distance / (2 * spread * spread)) / (np.float32(2.5066283) * spread)
    return matrix.astype(BF)


def column_taps():
    offsets = np.arange(2 * HALF + 1, dtype=np.float32) - HALF
    spread = np.float32(HALF / 2.0)
    weights = np.exp(-offsets * offsets / (2 * spread * spread))
    return weights / np.sum(weights)


def tap_matrix(width):
    rows = np.arange(width + LANES)
    place = np.where(rows < width + HALF, rows, rows - width - 2 * HALF)
    used = rows < width + 2 * HALF
    gap = place[:, None] - np.arange(width)[None, :]
    near = (np.abs(gap) <= HALF) & used[:, None]
    dense = np.where(near, column_taps()[np.clip(gap + HALF, 0, 2 * HALF)], 0.0).astype(np.float32)
    high = dense.astype(BF)
    low = (dense - high.astype(np.float32)).astype(BF)
    return high, low


def spread_levels(matrix):
    dense = np.kron(matrix.astype(np.float32), np.eye(PAIR, dtype=np.float32))
    return jnp.asarray(dense.astype(BF))


def dot(a, b):
    return jnp.dot(a, b, preferred_element_type=F32)


def greet(partners):
    barrier = pltpu.get_barrier_semaphore()
    for device in partners:
        pl.semaphore_signal(barrier, inc=1, device_id=device, device_id_type=MESH)
    return lambda: pl.semaphore_wait(barrier, len(partners))


def remote(src, dst, send_sem, recv_sem, device):
    return pltpu.make_async_remote_copy(
        src_ref=src,
        dst_ref=dst,
        send_sem=send_sem,
        recv_sem=recv_sem,
        device_id=device,
        device_id_type=MESH,
    )


def send(*args):
    copy = remote(*args)
    copy.start()
    return copy


def fetch(src, dst, sem):
    copy = pltpu.make_async_copy(src, dst, sem)
    copy.start()
    return copy


def others(axis, count):
    me = lax.axis_index(axis)
    return [lax.rem(me + k, count) for k in range(1, count)]


def flip(index):
    return index + 1 - 2 * lax.rem(index, 2)


def pack_edge(lane, part, shift):
    total = None
    for level in range(PAIR):
        moved = pltpu.roll(part(level), (2 * HALF * level + shift) % LANES, 1)
        total = moved if total is None else jnp.where(jnp.right_shift(lane, 3) == level, moved, total)
    return total


def unpack_edge(lane, packed, level):
    moved = pltpu.roll(packed, (LANES - 2 * HALF * level) % LANES, 1)
    return jnp.where(lane < 2 * HALF, moved, 0.0)


def front_kernel(
    levs,
    count,
    scale,
    ext_hbm,
    owner_hbm,
    control_hbm,
    members_hbm,
    kern_hbm,
    col_hbm,
    inn_hbm,
    w_hbm,
    cnt_hbm,
    kron_hbm,
    hi_hbm,
    lo_hbm,
    misfit_ref,
    mixed_all,
    mixed_low,
    mixed_rest,
    edge_all,
    ext_s,
    owner_s,
    control_v,
    members_v,
    kern_v,
    col_v,
    inn_v,
    w_v,
    cnt_v,
    kron_v,
    hi_v,
    lo_v,
    ctrl_all,
    ctrl_edge,
    mixed_v,
    mixed_own,
    edge_own,
    edge_out,
    edge_in,
    vert_v,
    field_all,
    field_v,
    part_v,
    chip_v,
    near_in,
    cross_out,
    cross_in,
    local_sem,
    ctl_sem,
    c_far,
    c_near,
    c_on,
    h_sem,
    f_sem,
    n_sem,
    x_sem,
    y_sem,
    m_far,
    m_near,
    m_on,
    m_loc,
):
    levels, members, width = control_v.shape
    tiles = width // LANES
    halves = members // PAIR
    blocks = col_v.shape[0]
    rows = blocks // levs
    lev, me = lax.axis_index("lev"), lax.axis_index("horiz")
    near, far = flip(lev), lax.rem(lev + 2, levs)
    across = flip(far)
    right, left = lax.rem(me + 1, count), lax.rem(me + count - 1, count)
    own = pl.ds(pl.multiple_of(lev * levels, levels), levels)
    afar = pl.ds(pl.multiple_of(far * levels, levels), levels)
    side, part = lax.rem(lev, 2), rows // 2

    tile_cols = [pl.ds(t * LANES, LANES) for t in range(tiles)]
    half_rows = [pl.ds(half * PAIR, PAIR) for half in range(halves)]
    all_here = greet(
        [{"lev": side} for side in others("lev", levs)]
        + [{"horiz": peer} for peer in others("horiz", count)]
    )
    ctl = [
        fetch(control_hbm.at[:, :, c], control_v.at[:, :, c], ctl_sem.at[t])
        for t, c in enumerate(tile_cols)
    ]
    away, beside, onward = {}, {}, {}

    def share(t, block):
        away[t] = send(block, block, c_far.at[0, t], c_far.at[1, t], {"lev": far})
        beside[t] = send(block, block, c_near.at[0, t], c_near.at[1, t], {"lev": near})

    def pass_on(t, block):
        away[t].wait_recv()
        onward[t] = send(block, block, c_on.at[0, t], c_on.at[1, t], {"lev": near})

    def share_tile(t):
        for half in range(halves):
            ctrl_all[half, own, :, tile_cols[t]] = control_v[:, half_rows[half], tile_cols[t]].astype(BF)
        share(t, ctrl_all.at[:, own, :, tile_cols[t]])

    lane = lax.broadcasted_iota(jnp.int32, (PAIR, LANES), 1)
    low_lane = jnp.bitwise_and(lane, 2 * HALF - 1)
    after = HALF * jnp.where(me < count - 1, 1, 0)
    before = HALF * jnp.where(me > 0, 1, 0)

    def send_edges(which, source):
        first, last = source.at[:, :, tile_cols[0]], source.at[:, :, tile_cols[tiles - 1]]
        copies = []
        for side, (view, shift, peer) in enumerate(((first, 0, left), (last, 2 * HALF, right))):
            for half in range(halves):
                packed = pack_edge(lane, lambda level: view[level, half_rows[half], :], shift)
                edge_out[which, side, half] = packed.astype(BF)
            copies.append(
                send(
                    edge_out.at[which, side],
                    edge_in.at[which, side],
                    h_sem.at[0, which, side],
                    h_sem.at[1, which, side],
                    {"horiz": peer},
                )
            )
        return copies

    def merged_edge(which, half):
        edge = jnp.where(low_lane < after, edge_in[which, 0, half].astype(F32), 0.0)
        return jnp.where(
            (low_lane >= HALF) & (low_lane < HALF + before),
            edge_in[which, 1, half].astype(F32),
            edge,
        ).astype(BF)

    early = tiles // 2
    all_here()
    ctl[0].wait()
    share_tile(0)
    local = [
        fetch(src, dst, local_sem.at[k])
        for k, (src, dst) in enumerate(
            [
                (ext_hbm, ext_s),
                (members_hbm, members_v),
                (
                    kron_hbm.at[pl.ds(pl.multiple_of(lev * levels * PAIR, levels * PAIR), levels * PAIR)],
                    kron_v,
                ),
                (hi_hbm, hi_v),
                (lo_hbm, lo_v),
                (owner_hbm, owner_s),
                (kern_hbm, kern_v),
                (col_hbm, col_v),
                (inn_hbm, inn_v),
                (w_hbm, w_v),
                (cnt_hbm, cnt_v),
            ]
        )
    ]
    for t in range(1, tiles):
        ctl[t].wait()
        if t < early:
            share_tile(t)
    control_edges = send_edges(0, control_v)

    local[0].wait()
    local[1].wait()
    for t in range(tiles):
        total = ext_s[0] * members_v[:, 0, :, tile_cols[t]].astype(F32)
        for species in range(1, members_v.shape[1]):
            total = total + ext_s[species] * members_v[:, species, :, tile_cols[t]].astype(F32)
        mixed_v[:, :, tile_cols[t]] = total
        for half in range(halves):
            mixed_own[half, :, :, tile_cols[t]] = total[:, half * PAIR : (half + 1) * PAIR].astype(BF)
    mixed_edges = send_edges(1, mixed_v)

    for copy in control_edges:
        copy.wait_recv()
    for half in range(halves):
        ctrl_edge[lev, half] = merged_edge(0, half)
    share(tiles, ctrl_edge.at[lev])
    for t in range(early, tiles):
        share_tile(t)
    for copy in mixed_edges:
        copy.wait_recv()
    for half in range(halves):
        edge_own[half] = merged_edge(1, half)

    for k in range(2, 5):
        local[k].wait()

    def raise_tile(t):
        pass_on(t, ctrl_all.at[:, afar, :, tile_cols[t]])
        if t == tiles - 1:
            start_mixed()
        beside[t].wait_recv()
        onward[t].wait_recv()
        for half in range(halves):
            x = ctrl_all[half, :, :, tile_cols[t]].reshape(LEV * PAIR, LANES)
            vert_v[half, :, tile_cols[t]] = dot(kron_v[...], x).astype(BF)

    def raise_edge():
        pass_on(tiles, ctrl_edge.at[far])
        beside[tiles].wait_recv()
        onward[tiles].wait_recv()
        for half in range(halves):
            x = []
            for slab in range(levs):
                packed = ctrl_edge[slab, half].astype(F32)
                x += [unpack_edge(lane, packed, level).astype(BF) for level in range(levels)]
            x = jnp.concatenate(x, axis=0)
            vert_v[half, :, pl.ds(width, LANES)] = dot(kron_v[...], x).astype(BF)

    m_away, m_beside, m_onward, m_kept = [], [], [], []

    def start_mixed():
        cut = levels // 2
        rest = mixed_own.at[halves - 1, pl.ds(cut, cut)]
        m_kept.append(fetch(rest, mixed_rest, m_loc.at[halves + 1]))
        parts = [(mixed_own.at[half], mixed_all.at[half, own]) for half in range(halves - 1)]
        parts.append((mixed_own.at[halves - 1, pl.ds(0, cut)], mixed_low.at[lev]))
        parts.append((edge_own, edge_all.at[lev]))
        for k, (block, place) in enumerate(parts):
            m_away.append(send(block, place, m_far.at[0, k], m_far.at[1, k], {"lev": far}))
            m_beside.append(send(block, place, m_near.at[0, k], m_near.at[1, k], {"lev": near}))
            m_kept.append(fetch(block, place, m_loc.at[k]))

    f_copies = {}

    def make_field(t):
        spans = [pl.ds(max(t - 1, 0) * LANES, (min(t + 2, tiles) - max(t - 1, 0)) * LANES)]
        if t in (0, tiles - 1):
            spans.append(pl.ds(width, LANES))
        total = None
        for half in range(halves):
            inc = None
            for cols in spans:
                v = vert_v[half, :, cols]
                term = dot(v, hi_v[cols, tile_cols[t]]) + dot(v, lo_v[cols, tile_cols[t]])
                inc = term if inc is None else inc + term
            inc = inc.reshape(levels, PAIR, LANES)
            term = jnp.sum(mixed_v[:, half_rows[half], tile_cols[t]] * inc, axis=1)
            total = term if total is None else total + term
        field_all[me, t] = (total * scale).astype(BF)

    def send_field(group):
        block = field_all.at[me, pl.ds(group[0], len(group))]
        f_copies[group] = [
            send(
                block, block, f_sem.at[0, group[0], k], f_sem.at[1, group[0], k], {"horiz": peer}
            )
            for k, peer in enumerate(others("horiz", count))
        ]

    def take_field(group):
        for copy in f_copies[group]:
            copy.wait_recv()
        for t in group:
            for h in range(count):
                field_v[h, t] = field_all[h, t].astype(F32)

    def forward(peer, chosen, first):
        start = pl.multiple_of(peer * rows, rows)

        def step(group, carry):
            base = pl.multiple_of(start + group * GROUP, GROUP)
            cols = col_v[pl.ds(base, GROUP), :]
            out = []
            for i in range(GROUP):
                owner = owner_s[base + i]
                col = jnp.broadcast_to(cols[i : i + 1, :], (levels, LANES))
                low = jnp.bitwise_and(col, LANES - 1)
                high = jnp.right_shift(col, 7)
                picked = 0.0
                for tile in chosen:
                    value = jnp.take_along_axis(field_v[owner, tile], low, axis=1)
                    picked = jnp.where(high == tile, value, picked)
                prod = picked * kern_v[base + i].astype(F32)
                out.append(jnp.sum(prod, axis=0, keepdims=True))
            value = jnp.concatenate(out, axis=0)
            if not first:
                value = value + part_v[pl.ds(base, GROUP), :]
            part_v[pl.ds(base, GROUP), :] = value
            return carry

        lax.fori_loop(0, rows // GROUP, step, 0)

    def forward_all(chosen, first):
        lax.fori_loop(0, levs, lambda k, carry: (forward(k, chosen, first), carry)[1], 0)

    one, two = tuple(range(early)), tuple(range(early, tiles))
    raise_tile(0)
    raise_edge()
    raise_tile(1)
    make_field(0)
    for k in range(5, 8):
        local[k].wait()
    for t in range(2, tiles):
        raise_tile(t)
        make_field(t - 1)
        if t == early:
            send_field(one)
    make_field(tiles - 1)
    send_field(two)
    take_field(one)
    forward_all(one, True)
    take_field(two)

    def span(k):
        return pl.ds(pl.multiple_of(k * rows, rows), rows)

    def near_copy(k):
        return remote(
            part_v.at[span(k)], near_in.at[k], n_sem.at[0, k], n_sem.at[1, k], {"lev": near}
        )

    def cross_copy(k):
        return remote(
            cross_out.at[k], cross_in.at[k, side], x_sem.at[0, k], x_sem.at[1, k], {"lev": far}
        )

    def hand_copy(k):
        block = cross_in.at[k, side]
        return remote(block, block, y_sem.at[0, k], y_sem.at[1, k], {"lev": near})

    def sum_chip(k):
        near_copy(k).wait_recv()
        chip_v[span(k), :] = part_v[span(k), :] + near_in[k]
        own_part = pl.ds(pl.multiple_of(k * rows + side * part, part), part)
        cross_out[k] = chip_v[own_part, :].astype(BF)
        cross_copy(k).start()

    def hand_on(k):
        cross_copy(k).wait_recv()
        hand_copy(k).start()

    def one_part(k, carry):
        forward(k, two, False)
        near_copy(k).start()

        @pl.when(k >= 1)
        def _():
            sum_chip(k - 1)

        @pl.when(k >= 3)
        def _():
            hand_on(k - 3)

        return carry

    lax.fori_loop(0, levs, one_part, 0)
    sum_chip(levs - 1)

    for k in range(8, 11):
        local[k].wait()

    lane_row = lax.broadcasted_iota(jnp.int32, (rows, LANES), 1).astype(F32)
    for k in range(levs):
        if k >= levs - 3:
            hand_on(k)
    places = [mixed_all.at[half, afar] for half in range(halves - 1)]
    places += [mixed_low.at[far], edge_all.at[far]]
    for k, place in enumerate(places):
        m_away[k].wait_recv()
        m_onward.append(send(place, place, m_on.at[0, k], m_on.at[1, k], {"lev": near}))
    for k in range(levs):
        hand_copy(k).wait_recv()
        other = jnp.concatenate([cross_in[k, 0], cross_in[k, 1]], axis=0).astype(F32)
        evolved = chip_v[pl.ds(k * rows, rows), :] + other
        block = pl.ds(k * rows, rows)
        misfit = w_v[block, :].astype(F32) * (evolved - inn_v[block, :].astype(F32)) * scale
        counts = jnp.broadcast_to(cnt_v[pl.ds(k, 1), :].astype(F32), (LANES, LANES))
        live = lane_row < jnp.transpose(counts)
        misfit_ref[block, :] = jnp.where(live, misfit, 0.0).astype(BF)

    for k in range(levs):
        near_copy(k).wait_send()
        cross_copy(k).wait_send()
        hand_copy(k).wait_send()
    for copies in f_copies.values():
        for copy in copies:
            copy.wait_send()
    for group in (away, beside, onward):
        for copy in group.values():
            copy.wait_send()
    for copy in control_edges + mixed_edges + m_away:
        copy.wait_send()
    for copy in m_beside + m_onward + m_kept:
        copy.wait()


def adjoint_kernel(owner_ref, kern_ref, col_ref, mis_ref, out_ref, acc):
    blocks = col_ref.shape[0]
    levels = kern_ref.shape[1]
    count = acc.shape[0]
    tiles = acc.shape[2] // levels
    acc[...] = jnp.zeros_like(acc)
    lane_row = lax.broadcasted_iota(jnp.int32, (LANES, LANES), 0).astype(F32).astype(BF)
    one, zero = jnp.ones((), BF), jnp.zeros((), BF)

    def step(group, carry):
        base = pl.multiple_of(group * MANY, MANY)
        cols = col_ref[pl.ds(base, MANY), :]
        low = jnp.bitwise_and(cols, LANES - 1).astype(F32)
        high = jnp.right_shift(cols, 7)
        misfit = mis_ref[pl.ds(base, MANY), :].astype(F32)
        parts = [jnp.where(high == tile, misfit, 0.0) for tile in range(tiles)]
        for i in range(MANY):
            owner = owner_ref[base + i]
            kern = kern_ref[base + i]
            rows = jnp.concatenate(
                [
                    kern * jnp.broadcast_to(part[i : i + 1, :], (levels, LANES)).astype(BF)
                    for part in parts
                ],
                axis=0,
            )
            row = jnp.broadcast_to(low[i : i + 1, :], (LANES, LANES)).astype(BF)
            hot = jnp.where(lane_row == row, one, zero)
            acc[owner] += lax.dot_general(
                hot, rows, (((1,), (1,)), ((), ())), preferred_element_type=F32
            )
        return carry

    lax.fori_loop(0, blocks // MANY, step, 0)

    lane = lax.broadcasted_iota(jnp.int32, (levels, LANES), 1)
    sums = [jnp.transpose(acc[h]) for h in range(count)]
    for h in range(count):
        out_ref[h, pl.ds(0, tiles * levels)] = sums[h].astype(BF)
        edge = jnp.zeros((levels, LANES), F32)
        if h < count - 1:
            edge = jnp.where(lane < HALF, sums[h + 1][:levels], edge)
        if h > 0:
            moved = pltpu.roll(sums[h - 1][(tiles - 1) * levels :], 2 * HALF, 1)
            edge = jnp.where((lane >= HALF) & (lane < 2 * HALF), moved, edge)
        out_ref[h, pl.ds(tiles * levels, levels)] = edge.astype(BF)


def back_kernel(
    count,
    levs,
    x_ref,
    mixed_hbm,
    low_hbm,
    rest_hbm,
    edge_hbm,
    kron_hbm,
    out_ref,
    mixed_v,
    low_v,
    rest_v,
    edge_v,
    kron_v,
    fg_v,
    slots,
    r_sem,
    a_sem,
    m_sem,
    local_sem,
):
    halves, size, full = out_ref.shape
    levels = size // PAIR
    tiles = full // LANES
    early = (tiles - 1) // 2
    groups = [range(early), range(early, tiles)]
    rows = [pl.ds(group[0] * levels, len(group) * levels) for group in groups]
    me, lev = lax.axis_index("horiz"), lax.axis_index("lev")
    near, far = flip(lev), lax.rem(lev + 2, levs)
    sides = [near, far, flip(far)]
    peers = others("horiz", count)
    greet([{"horiz": peer} for peer in peers] + [{"lev": side} for side in sides])()
    reduce = [
        [
            send(
                x_ref.at[peer, part],
                slots.at[k, part],
                r_sem.at[0, g, k],
                r_sem.at[1, g, k],
                {"horiz": peer},
            )
            for k, peer in enumerate(peers)
        ]
        for g, part in enumerate(rows)
    ]
    place = rest_v.at[lev]
    m_away = send(rest_hbm, place, m_sem.at[0, 0], m_sem.at[1, 0], {"lev": far})
    m_beside = send(rest_hbm, place, m_sem.at[0, 1], m_sem.at[1, 1], {"lev": near})
    at = pl.multiple_of(lev * size, size)
    local = [
        fetch(mixed_hbm, mixed_v, local_sem.at[0]),
        fetch(edge_hbm, edge_v, local_sem.at[1]),
        fetch(kron_hbm.at[pl.ds(at, size)], kron_v, local_sem.at[2]),
        fetch(low_hbm, low_v, local_sem.at[3]),
        fetch(rest_hbm, rest_v.at[lev], local_sem.at[4]),
    ]
    lane = lax.broadcasted_iota(jnp.int32, (PAIR, LANES), 1)

    def total_up(g):
        part = rows[g]
        total = x_ref[me, part].astype(F32)
        for k, copy in enumerate(reduce[g]):
            copy.wait_recv()
            total = total + slots[k, part].astype(F32)
        fg_v[lev, part] = total
        block = fg_v.at[lev, part]
        return [
            send(block, block, a_sem.at[0, g, k], a_sem.at[1, g, k], {"lev": side})
            for k, side in enumerate(sides)
        ]

    def slab(index, g, first):
        start = pl.multiple_of(index * levels, levels)
        begin = pl.multiple_of(index * size, size)
        group = groups[g]
        span = pl.ds(group[0] * LANES, len(group) * LANES)
        for half in range(halves):
            columns = []
            for t in group:
                fg = fg_v[index, pl.ds(t * levels, levels), :]
                if t < tiles - 1:
                    cols = pl.ds(t * LANES, LANES)
                    if half < halves - 1:
                        m = mixed_v[half, pl.ds(start, levels), :, cols]
                    else:
                        m = jnp.concatenate(
                            [low_v[index, :, :, cols], rest_v[index, :, :, cols]], axis=0
                        )
                    grad = (m.astype(F32) * fg[:, None, :]).astype(BF).reshape(size, LANES)
                else:
                    packed = edge_v[index, half].astype(F32)
                    grad = jnp.concatenate(
                        [
                            (unpack_edge(lane, packed, level) * fg[level : level + 1, :]).astype(BF)
                            for level in range(levels)
                        ],
                        axis=0,
                    )
                columns.append(grad)
            term = dot(kron_v[:, pl.ds(begin, size)], jnp.concatenate(columns, axis=1))
            out_ref[half, :, span] = term if first else out_ref[half, :, span] + term

    spread = [total_up(0)]
    for copy in local:
        copy.wait()
    slab(lev, 0, True)
    m_away.wait_recv()
    place = rest_v.at[far]
    m_onward = send(place, place, m_sem.at[0, 2], m_sem.at[1, 2], {"lev": near})
    spread.append(total_up(1))
    slab(lev, 1, True)
    for g in range(2):
        for k, side in enumerate(sides):
            spread[g][k].wait_recv()
            if g == 0 and k != 1:
                (m_onward if k else m_beside).wait_recv()
            slab(side, g, False)
    for copies in reduce + spread + [[m_away, m_beside, m_onward]]:
        for copy in copies:
            copy.wait_send()


def final_kernel(levels_ref, hi_ref, lo_ref, control_ref, out_hbm, out_v, sem):
    levels, members, width = control_ref.shape
    copies = []
    for half in range(members // PAIR):
        part = pl.ds(half * PAIR, PAIR)
        mixed_levels = levels_ref[half]
        high = mixed_levels.astype(BF)
        low = (mixed_levels - high.astype(F32)).astype(BF)
        total = dot(high, hi_ref[...]) + dot(high, lo_ref[...]) + dot(low, hi_ref[...])
        out_v[half] = control_ref[:, part, :] + total.reshape(levels, PAIR, width)
        copies.append(fetch(out_v.at[half], out_hbm.at[:, part, :], sem.at[half]))
    for copy in copies:
        copy.wait()


def vmem(count):
    return [pl.BlockSpec(memory_space=pltpu.VMEM)] * count


def smem(count):
    return [pl.BlockSpec(memory_space=pltpu.SMEM)] * count


def hbm(count):
    return [pl.BlockSpec(memory_space=pltpu.HBM)] * count


def pairs(*size):
    return pltpu.SemaphoreType.DMA((2,) + size)


def body(
    control,
    members,
    extinction,
    kernels,
    innovation,
    obs_weight,
    owners,
    pixel_columns,
    pixel_counts,
):
    levels, mem_count, width = control.shape
    blocks, _, pixels = kernels.shape
    count, levs = lax.axis_size("horiz"), lax.axis_size("lev")
    tiles = width // LANES
    halves = mem_count // PAIR
    rows = blocks // levs
    full = width + LANES
    kron_all = spread_levels(level_matrix())
    high, low = tap_matrix(width)
    hi, lo = jnp.asarray(high), jnp.asarray(low)
    scale = 1.0 / math.sqrt(mem_count)
    owner_ids = owners[:, 0]

    misfit, mixed_all, mixed_low, mixed_rest, edge_all = pl.pallas_call(
        functools.partial(front_kernel, levs, count, scale),
        out_shape=[
            jax.ShapeDtypeStruct((blocks, pixels), BF),
            jax.ShapeDtypeStruct((halves - 1, levs * levels, PAIR, width), BF),
            jax.ShapeDtypeStruct((levs, levels // 2, PAIR, width), BF),
            jax.ShapeDtypeStruct((levels // 2, PAIR, width), BF),
            jax.ShapeDtypeStruct((levs, halves, PAIR, LANES), BF),
        ],
        in_specs=hbm(12),
        out_specs=vmem(1) + hbm(4),
        scratch_shapes=[
            pltpu.SMEM(extinction.shape, F32),
            pltpu.SMEM(owner_ids.shape, jnp.int32),
            pltpu.VMEM(control.shape, F32),
            pltpu.VMEM(members.shape, BF),
            pltpu.VMEM(kernels.shape, BF),
            pltpu.VMEM(pixel_columns.shape, jnp.int32),
            pltpu.VMEM((blocks, pixels), BF),
            pltpu.VMEM((blocks, pixels), BF),
            pltpu.VMEM((levs, rows), jnp.int32),
            pltpu.VMEM((levels * PAIR, LEV * PAIR), BF),
            pltpu.VMEM((full, width), BF),
            pltpu.VMEM((full, width), BF),
            pltpu.VMEM((halves, levs * levels, PAIR, width), BF),
            pltpu.VMEM((levs, halves, PAIR, LANES), BF),
            pltpu.VMEM((levels, mem_count, width), F32),
            pltpu.VMEM((halves, levels, PAIR, width), BF),
            pltpu.VMEM((halves, PAIR, LANES), BF),
            pltpu.VMEM((2, 2, halves, PAIR, LANES), BF),
            pltpu.VMEM((2, 2, halves, PAIR, LANES), BF),
            pltpu.VMEM((halves, levels * PAIR, full), BF),
            pltpu.VMEM((count, tiles, levels, LANES), BF),
            pltpu.VMEM((count, tiles, levels, LANES), F32),
            pltpu.VMEM((blocks, pixels), F32),
            pltpu.VMEM((blocks, pixels), F32),
            pltpu.VMEM((levs, rows, pixels), F32),
            pltpu.VMEM((levs, rows // 2, pixels), BF),
            pltpu.VMEM((levs, 2, rows // 2, pixels), BF),
            pltpu.SemaphoreType.DMA((11,)),
            pltpu.SemaphoreType.DMA((tiles,)),
            pairs(tiles + 1),
            pairs(tiles + 1),
            pairs(tiles + 1),
            pairs(2, 2),
            pairs(tiles, count - 1),
            pairs(levs),
            pairs(levs),
            pairs(levs),
            pairs(halves + 1),
            pairs(halves + 1),
            pairs(halves + 1),
            pltpu.SemaphoreType.DMA((halves + 2,)),
        ],
        compiler_params=pltpu.CompilerParams(
            vmem_limit_bytes=58 * MIB, collective_id=0, has_side_effects=True
        ),
    )(
        extinction,
        owner_ids,
        control,
        members,
        kernels,
        pixel_columns,
        innovation,
        obs_weight,
        pixel_counts.reshape(levs, rows),
        kron_all,
        hi,
        lo,
    )

    partial = pl.pallas_call(
        adjoint_kernel,
        out_shape=jax.ShapeDtypeStruct((count, (tiles + 1) * levels, LANES), BF),
        in_specs=smem(1) + vmem(3),
        out_specs=pl.BlockSpec(memory_space=pltpu.VMEM),
        scratch_shapes=[pltpu.VMEM((count, LANES, tiles * levels), F32)],
        compiler_params=pltpu.CompilerParams(vmem_limit_bytes=32 * MIB),
    )(owner_ids, kernels, pixel_columns, misfit)

    levels_mixed = pl.pallas_call(
        functools.partial(back_kernel, count, levs),
        out_shape=jax.ShapeDtypeStruct((halves, levels * PAIR, full), F32),
        in_specs=vmem(1) + hbm(5),
        out_specs=pl.BlockSpec(memory_space=pltpu.VMEM),
        scratch_shapes=[
            pltpu.VMEM(mixed_all.shape, BF),
            pltpu.VMEM(mixed_low.shape, BF),
            pltpu.VMEM(mixed_low.shape, BF),
            pltpu.VMEM(edge_all.shape, BF),
            pltpu.VMEM((levels * PAIR, LEV * PAIR), BF),
            pltpu.VMEM((levs, (tiles + 1) * levels, LANES), F32),
            pltpu.VMEM((count - 1, (tiles + 1) * levels, LANES), BF),
            pairs(2, count - 1),
            pairs(2, levs - 1),
            pairs(3),
            pltpu.SemaphoreType.DMA((5,)),
        ],
        compiler_params=pltpu.CompilerParams(
            vmem_limit_bytes=50 * MIB, collective_id=1, has_side_effects=True
        ),
    )(partial, mixed_all, mixed_low, mixed_rest, edge_all, kron_all)

    return pl.pallas_call(
        final_kernel,
        out_shape=jax.ShapeDtypeStruct(control.shape, F32),
        in_specs=vmem(4),
        out_specs=pl.BlockSpec(memory_space=pltpu.HBM),
        scratch_shapes=[
            pltpu.VMEM((halves, levels, PAIR, width), F32),
            pltpu.SemaphoreType.DMA((halves,)),
        ],
        compiler_params=pltpu.CompilerParams(vmem_limit_bytes=32 * MIB),
    )(levels_mixed, hi, lo, control)


def solution(mesh):
    placed = (
        P("lev", None, "horiz"),
        P("lev", None, None, "horiz"),
        P(),
        P("horiz", "lev", None),
        P("horiz", None),
        P("horiz", None),
        P("horiz", None),
        P("horiz", None),
        P("horiz"),
    )
    return jax.shard_map(
        body, mesh=mesh, in_specs=placed, out_specs=P("lev", None, "horiz"), check_vma=False
    )
```
